32 devices in a mesh: groups: 2 (over x), tensor: 16 (over z, y, core).
Axes of the slice: x: 2, y: 2, z: 4, core: 2. Of those that a mesh axis runs over, the one named last changes fastest.
Arguments:
- gate_act: bfloat16 [53248, 32], P('tensor', 'groups'), parts along dimension 1, may hold values from -6 to 6
- up_act: bfloat16 [53248, 32], P('tensor', 'groups'), parts along dimension 1, may hold values from -6 to 6
- codes: int32 [26624, 8192], P('tensor'), may hold values from 0 to 255
- scales: bfloat16 [1664, 8192], P('tensor'), may hold values from 0.00039863586 to 0.0015945435
Outputs:
- ffn_out: bfloat16 [32, 8192], P(('groups', 'tensor')), parts along dimension 0
The draws below stay inside these ranges and needn't reach their ends.
There are 2 independent parts, one for each index of `groups`. The reference program is written for one: setup_inputs(seed, part) draws one part's arguments, and reference() takes and returns one part's arrays. A program takes and returns all parts, laid end to end along the dimension named above; an argument that names none is the same for every part. Nothing has to cross between parts.
Inputs may be any that keep to these rules, and one draw needn't show every extreme that they name: Each word packs two 4-bit codes as stated in the reference program.
All inputs are finite; a program needn't handle non-finite values.
Results may differ from the reference program's by a relative error of at most 0.007.
Values may be sent and summed in bfloat16 or wider, within the bound.
No kernel may reach another device: no remote copies, remote signals or barrier semaphores. Data moves between devices by JAX's collectives and lax.ppermute only.
A program may use at most 384 MiB of HBM per device.

```python
import math
import jax
import jax.numpy as jnp
import numpy as np
from jax import lax

D = 8192
FF = 53248
HAD_CROSS = 128
GROUP = 32
HAD_LOCAL = 416
ROWS = 16


def touch_ends(result, key, least, top_value):
    longest = result.shape.index(max(result.shape))
    spots = []
    for shift in (0, 1):
        where = [jax.random.randint(jax.random.fold_in(key, axis), (), 0, length) for axis, length in enumerate(result.shape)]
        where[longest] = (where[longest] + shift) % result.shape[longest]
        spots.append(tuple(where))
    return result.at[spots[0]].set(least).at[spots[1]].set(top_value)


def shard_levels(own_key, shape, cuts, smallest, largest):
    def one(axis_at, blocks):
        heights = jax.random.uniform(jax.random.fold_in(jax.random.fold_in(own_key, 6), axis_at), (blocks,), jnp.float32, smallest / len(cuts), largest / len(cuts))
        return jnp.repeat(jnp.exp(heights), shape[axis_at] // blocks).reshape((-1,) + (1,) * (len(shape) - axis_at - 1))

    factor_of = one(*cuts[0])
    for cut in cuts[1:]:
        factor_of = factor_of * one(*cut)
    return factor_of


def scatter_about(rng, extent, width, limit, cuts=(), kind=jnp.bfloat16):
    result = width * jax.random.normal(rng, extent, jnp.float32)
    if cuts:
        result = result * shard_levels(rng, extent, cuts, -0.22, 0.18)
    return jnp.clip(result, -limit, limit).astype(kind)


def setup_inputs(seed: int = 0, part: int = 0) -> dict:
    streams_of = jax.random.split(jax.random.key(seed), 5)
    part_keys = jax.random.split(jax.random.fold_in(streams_of[4], part), 5)
    gate_act = scatter_about(part_keys[0], (FF, ROWS), 1.0, 6.0, ((0, 16),))
    up_act = scatter_about(part_keys[1], (FF, ROWS), 1.0, 6.0, ((0, 16),))
    codes = touch_ends(jax.random.randint(streams_of[2], (FF // 2, D), 0, 256), jax.random.fold_in(streams_of[2], 1), 0, 255).astype(jnp.int32)
    scales = jnp.clip(jnp.exp(math.log(0.0015945435) - 1.3862944 * jax.random.uniform(streams_of[3], (FF // GROUP, D), jnp.float32) ** shard_levels(streams_of[3], (FF // GROUP, D), ((0, 16),), -0.2, 0.2)), 0.00039863586, 0.0015945435).astype(jnp.bfloat16)
    return dict(gate_act=gate_act, up_act=up_act, codes=codes, scales=scales)


def paley_table():
    squares = set()
    for real_part in range(5):
        for root_part in range(5):
            squares.add(((real_part * real_part + 2 * root_part * root_part) % 5, 2 * real_part * root_part % 5))
    jacobsthal = np.zeros((25, 25))
    for first in range(25):
        for second in range(25):
            differ = ((first // 5 - second // 5) % 5, (first % 5 - second % 5) % 5)
            if differ == (0, 0):
                jacobsthal[first, second] = 0.0
            elif differ in squares:
                jacobsthal[first, second] = 1.0
            else:
                jacobsthal[first, second] = -1.0
    conference = np.zeros((26, 26))
    conference[0, 1:] = 1.0
    conference[1:, 0] = 1.0
    conference[1:, 1:] = jacobsthal
    return np.kron(conference, np.array([[1.0, 1.0], [1.0, -1.0]])) + np.kron(np.eye(26), np.array([[1.0, -1.0], [-1.0, -1.0]]))

def walsh_table(order):
    matrix = np.ones((1, 1))
    while matrix.shape[0] < order:
        matrix = np.kron(np.array([[1.0, 1.0], [1.0, -1.0]]), matrix)
    return matrix

def hadamard_local(order):
    matrix = np.kron(walsh_table(order // 52), paley_table()) / math.sqrt(order)
    return jnp.asarray(matrix, dtype=jnp.float32).astype(jnp.bfloat16)

def sign_table(order):
    row_index = jnp.arange(order, dtype=jnp.int32)[:, None]
    col_index = jnp.arange(order, dtype=jnp.int32)[None, :]
    shared = jnp.zeros((order, order), jnp.int32)
    for bit_pos in range(order.bit_length() - 1):
        shared = shared + row_index // 2 ** bit_pos % 2 * (col_index // 2 ** bit_pos % 2)
    return (1 - 2 * (shared % 2)).astype(jnp.float32)

def dequantize(words, group_scales):
    low_codes = words % 16
    high_codes = words // 16
    unpacked = jnp.stack([low_codes, high_codes], axis=1).reshape(2 * words.shape[0], words.shape[1])
    spread = jnp.repeat(group_scales.astype(jnp.float32), GROUP, axis=0)
    return ((unpacked - 8).astype(jnp.float32) * spread).astype(jnp.bfloat16)

def reference(gate_act, up_act, codes, scales):
    total_rows = gate_act.shape[1]
    hidden = (jax.nn.silu(gate_act.astype(jnp.float32)) * up_act.astype(jnp.float32)).astype(jnp.bfloat16)
    blocks = hidden.reshape(HAD_CROSS, HAD_LOCAL, total_rows)
    local_table = hadamard_local(HAD_LOCAL).astype(jnp.float32)
    local = jnp.einsum('kn,anr->akr', local_table, blocks.astype(jnp.float32), precision=lax.Precision.HIGHEST).astype(jnp.bfloat16)
    signs = sign_table(HAD_CROSS)
    rotated = (jnp.einsum('abr,ae->ebr', local.astype(jnp.float32), signs, precision=lax.Precision.HIGHEST) * (1.0 / math.sqrt(HAD_CROSS))).astype(jnp.bfloat16)
    word_blocks = codes.reshape(HAD_CROSS, HAD_LOCAL // 2, codes.shape[1])
    scale_blocks = scales.reshape(HAD_CROSS, HAD_LOCAL // GROUP, scales.shape[1])

    def advance(total, items):
        words, group_scales, values = items
        weight = dequantize(words, group_scales)
        return (total + jnp.dot(values.T, weight, preferred_element_type=jnp.float32), None)
    start = jnp.zeros((total_rows, codes.shape[1]), jnp.float32)
    total, unused = lax.scan(advance, start, (word_blocks, scale_blocks, rotated))
    return total.astype(jnp.bfloat16)
```

```python
import functools
import math

import jax
import jax.numpy as jnp
import numpy as np
from jax import lax
from jax.experimental import pallas as pl
from jax.experimental.pallas import tpu as pltpu
from jax.sharding import PartitionSpec as P

HAD_CROSS = 128
GROUP = 32
HAD_LOCAL = 416
PAIRS = HAD_LOCAL // 2
WORDS_PER_GROUP = GROUP // 2
AXES = ("groups", "tensor")
MIB = 2**20


def paley_table():
    squares = set()
    for real_part in range(5):
        for root_part in range(5):
            squares.add(
                (
                    (real_part * real_part + 2 * root_part * root_part) % 5,
                    2 * real_part * root_part % 5,
                )
            )
    jacobsthal = np.zeros((25, 25))
    for first in range(25):
        for second in range(25):
            differ = ((first // 5 - second // 5) % 5, (first % 5 - second % 5) % 5)
            if differ == (0, 0):
                jacobsthal[first, second] = 0.0
            elif differ in squares:
                jacobsthal[first, second] = 1.0
            else:
                jacobsthal[first, second] = -1.0
    conference = np.zeros((26, 26))
    conference[0, 1:] = 1.0
    conference[1:, 0] = 1.0
    conference[1:, 1:] = jacobsthal
    return np.kron(conference, np.array([[1.0, 1.0], [1.0, -1.0]])) + np.kron(
        np.eye(26), np.array([[1.0, -1.0], [-1.0, -1.0]])
    )


def walsh_table(order):
    matrix = np.ones((1, 1))
    while matrix.shape[0] < order:
        matrix = np.kron(np.array([[1.0, 1.0], [1.0, -1.0]]), matrix)
    return matrix


def local_matrix(order):
    return np.kron(walsh_table(order // 52), paley_table()) / math.sqrt(order)


def hadamard_local(order):
    return jnp.asarray(local_matrix(order), dtype=jnp.float32).astype(jnp.bfloat16)


def sign_table(order):
    return jnp.asarray(walsh_table(order), dtype=jnp.float32)


def swapped(value, axis, distance):
    mask = 2**distance
    pairs = [(source, source ^ mask) for source in range(lax.axis_size(axis))]
    return lax.ppermute(value, axis, pairs)


def dequantize(words, group_scales):
    low_codes = words % 16
    high_codes = words // 16
    unpacked = jnp.stack([low_codes, high_codes], axis=1).reshape(
        2 * words.shape[0], words.shape[1]
    )
    spread = jnp.repeat(group_scales.astype(jnp.float32), GROUP, axis=0)
    return ((unpacked - 8).astype(jnp.float32) * spread).astype(jnp.bfloat16)


def general_body(gate_act, up_act, codes, scales):
    units_here = gate_act.shape[0]
    total_rows = gate_act.shape[1]
    blocks_here = units_here // HAD_LOCAL
    factor = 1.0 / math.sqrt(HAD_CROSS)
    hidden = (jax.nn.silu(gate_act.astype(jnp.float32)) * up_act.astype(jnp.float32)).astype(
        jnp.bfloat16
    )
    hidden = hidden.reshape(blocks_here, HAD_LOCAL, total_rows)
    local = jnp.einsum(
        "kn,anr->akr", hadamard_local(HAD_LOCAL), hidden, preferred_element_type=jnp.float32
    ).astype(jnp.bfloat16)
    partial_sums = jnp.einsum(
        "abr,ae->ebr",
        local.astype(jnp.float32),
        sign_table(blocks_here),
        precision=lax.Precision.HIGHEST,
    )
    my_index = lax.axis_index("tensor")
    for bit_pos in range(lax.axis_size("tensor").bit_length() - 1):
        partner = swapped(partial_sums, "tensor", bit_pos)
        upper = my_index // 2**bit_pos % 2
        partial_sums = jnp.where(upper == 0, partial_sums + partner, partner - partial_sums)
    rotated = (partial_sums * factor).astype(jnp.bfloat16)
    rotated = rotated.reshape(units_here, total_rows)
    weight = dequantize(codes, scales)
    summed = lax.psum_scatter(
        lax.dot_general(
            rotated, weight, (((0,), (0,)), ((), ())), preferred_element_type=jnp.float32
        ),
        "tensor",
        scatter_dimension=0,
        tiled=True,
    )
    return summed.astype(jnp.bfloat16)


def exchanged(value, group_mask, tensor_mask):
    tensor_size = lax.axis_size("tensor")
    pairs = [
        (g * tensor_size + t, (g ^ group_mask) * tensor_size + (t ^ tensor_mask))
        for g in range(lax.axis_size("groups"))
        for t in range(tensor_size)
    ]
    return lax.ppermute(value, AXES, pairs)


def parity_sign(bits, masks):
    total = jnp.int32(0)
    position = 1
    while position <= masks:
        if masks & position:
            total = total + bits // position % 2
        position *= 2
    return (1 - 2 * (total % 2)).astype(jnp.float32)


def local_kernel(group_ref, gate_ref, up_ref, table_ref, walsh_ref, out_ref, gate_sc, up_sc, mix_sc):
    rows = gate_ref.shape[1]
    blocks = gate_ref.shape[0] // HAD_LOCAL
    half = blocks // 2
    for a in range(blocks):
        here = slice(a * HAD_LOCAL, (a + 1) * HAD_LOCAL)
        there = slice(a * rows, (a + 1) * rows)
        gate_sc[:, there] = gate_ref[here, :].astype(jnp.float32)
        up_sc[:, there] = up_ref[here, :].astype(jnp.float32)
    gate = gate_sc[...]
    hidden = (gate / (1.0 + jnp.exp(-gate)) * up_sc[...]).astype(jnp.bfloat16)
    local = lax.dot_general(
        hidden, table_ref[...], (((0,), (0,)), ((), ())), preferred_element_type=jnp.float32
    ).astype(jnp.bfloat16)
    mix_sc[...] = jnp.dot(walsh_ref[...], local, preferred_element_type=jnp.float32).astype(
        jnp.bfloat16
    )
    padded = table_ref.shape[1] // 2
    group = group_ref[0]
    for part in range(2):
        first = (group if part == 0 else 1 - group) * half
        for parity in range(2):
            for e in range(half):
                start = pl.multiple_of((first + e) * rows, rows)
                offset = (parity * half + e) * PAIRS
                out_ref[part, :, offset : offset + PAIRS] = mix_sc[
                    pl.ds(start, rows), parity * padded : parity * padded + PAIRS
                ]


def local_rotation(group, gate_act, up_act):
    units, rows = gate_act.shape
    blocks = units // HAD_LOCAL
    padded = -(-PAIRS // 128) * 128
    by_parity = local_matrix(HAD_LOCAL).reshape(PAIRS, 2, HAD_LOCAL)
    table = np.zeros((HAD_LOCAL, 2 * padded), np.float32)
    table[:, :PAIRS] = by_parity[:, 0].T
    table[:, padded : padded + PAIRS] = by_parity[:, 1].T
    walsh = np.kron(walsh_table(blocks), np.eye(rows))
    whole = pl.BlockSpec(memory_space=pltpu.VMEM)
    return pl.pallas_call(
        local_kernel,
        in_specs=[pl.BlockSpec(memory_space=pltpu.SMEM)] + [whole] * 4,
        out_specs=whole,
        out_shape=jax.ShapeDtypeStruct((2, rows, units // 2), jnp.bfloat16),
        scratch_shapes=[
            pltpu.VMEM((HAD_LOCAL, blocks * rows), jnp.float32),
            pltpu.VMEM((HAD_LOCAL, blocks * rows), jnp.float32),
            pltpu.VMEM((blocks * rows, 2 * padded), jnp.bfloat16),
        ],
        compiler_params=pltpu.CompilerParams(vmem_limit_bytes=8 * MIB),
        cost_estimate=pl.CostEstimate(flops=10**8, bytes_accessed=2 * MIB, transcendentals=10**5),
        name="local_rotation",
    )(
        group,
        gate_act,
        up_act,
        jnp.asarray(table, jnp.bfloat16),
        jnp.asarray(walsh, jnp.bfloat16),
    )


def unpack_kernel(tile, group_ref, codes_ref, scales_ref, out_ref, scales_sc):
    step = pl.program_id(0)
    rows, columns = codes_ref.shape
    steps = pl.num_programs(0)
    spans = rows // WORDS_PER_GROUP
    plane = out_ref.shape[0] // 2

    @pl.when(step == 0)
    def _():
        scales_sc[...] = scales_ref[...].astype(jnp.float32)

    first = (group_ref[0] * steps + step) * spans
    for p in range(spans):
        for q in range(0, columns, tile):
            words = codes_ref[p * WORDS_PER_GROUP : (p + 1) * WORDS_PER_GROUP, q : q + tile]
            scale = scales_sc[pl.ds(first + p, 1), q : q + tile]
            low = ((words & 15) - 8).astype(jnp.float32) * scale
            high = ((words >> 4) - 8).astype(jnp.float32) * scale
            at = pl.multiple_of(step * rows + p * WORDS_PER_GROUP, WORDS_PER_GROUP)
            out_ref[pl.ds(at, WORDS_PER_GROUP), q : q + tile] = low.astype(jnp.bfloat16)
            at = pl.multiple_of(plane + step * rows + p * WORDS_PER_GROUP, WORDS_PER_GROUP)
            out_ref[pl.ds(at, WORDS_PER_GROUP), q : q + tile] = high.astype(jnp.bfloat16)


def unpack(group, codes, scales, chunk, columns):
    words = codes.shape[0]
    steps = words // PAIRS // 2
    return pl.pallas_call(
        functools.partial(unpack_kernel, 512),
        grid_spec=pltpu.PrefetchScalarGridSpec(
            num_scalar_prefetch=1,
            grid=(steps,),
            in_specs=[
                pl.BlockSpec((PAIRS, columns), lambda i, g: (g[0] * steps + i, chunk)),
                pl.BlockSpec((scales.shape[0], columns), lambda i, g: (0, chunk)),
            ],
            out_specs=pl.BlockSpec(memory_space=pltpu.VMEM),
            scratch_shapes=[pltpu.VMEM((scales.shape[0], columns), jnp.float32)],
        ),
        out_shape=pltpu.VMEM((words, columns), jnp.bfloat16),
        compiler_params=pltpu.CompilerParams(vmem_limit_bytes=12 * MIB),
        cost_estimate=pl.CostEstimate(
            flops=words * columns * 8, bytes_accessed=words * columns * 4, transcendentals=0
        ),
        name=f"unpack_{chunk}",
    )(group, codes, scales)


def product_kernel(tile, chunks, place_ref, own_ref, *refs):
    others = refs[: len(refs) - chunks - 2]
    weights = refs[len(others) : len(others) + chunks]
    keep_ref, send_ref = refs[-2:]
    rows = own_ref.shape[0]
    place = place_ref[0]
    count = len(others) + 1
    far = 4 * (count - 1)
    total = own_ref[...].astype(jnp.float32) * parity_sign(place, far)
    for index, other in enumerate(others):
        total = total + other[...].astype(jnp.float32) * parity_sign(
            place & (place ^ (4 * (index + 1))), far
        )
    rotated = (total * (1.0 / math.sqrt(HAD_CROSS))).astype(jnp.bfloat16)
    each = rows // (8 * count)
    slot = lax.broadcasted_iota(jnp.int32, (rows, rows), 0)
    column = lax.broadcasted_iota(jnp.int32, (rows, rows), 1)
    unit = slot // each
    away = unit // (4 * count) + 2 * (unit // count % 2) + 4 * (unit % count)
    source = (unit // (2 * count) % 2) * (rows // 2) + (away ^ place) * each + slot % each
    pick = (column == source).astype(jnp.float32).astype(jnp.bfloat16)
    rotated = jnp.dot(pick, rotated, preferred_element_type=jnp.float32).astype(jnp.bfloat16)
    for index, weight in enumerate(weights):
        columns = weight.shape[1]

        @pl.loop(0, columns // tile)
        def _(i, weight=weight, index=index, columns=columns):
            at = pl.multiple_of(i * tile, tile)
            result = jnp.dot(
                rotated, weight[:, pl.ds(at, tile)], preferred_element_type=jnp.float32
            )
            to = pl.ds(pl.multiple_of(index * columns + at, tile), tile)
            keep_ref[:, to] = result[: rows // 2]
            send_ref[:, to] = result[rows // 2 :].astype(jnp.bfloat16)


def product(place, own, others, weights):
    rows = own.shape[0]
    width = sum(w.shape[1] for w in weights)
    whole = pl.BlockSpec(memory_space=pltpu.VMEM)
    weights = [pltpu.with_memory_space_constraint(w, pltpu.VMEM) for w in weights]
    return pl.pallas_call(
        functools.partial(product_kernel, 512, len(weights)),
        in_specs=[pl.BlockSpec(memory_space=pltpu.SMEM)]
        + [whole] * (1 + len(others) + len(weights)),
        out_specs=[whole, whole],
        out_shape=[
            jax.ShapeDtypeStruct((rows // 2, width), jnp.float32),
            jax.ShapeDtypeStruct((rows // 2, width), jnp.bfloat16),
        ],
        compiler_params=pltpu.CompilerParams(vmem_limit_bytes=8 * MIB),
        name="product",
    )(place, own, *others, *weights)


def shared_body(gate_act, up_act, codes, scales):
    rows = gate_act.shape[1]
    width = codes.shape[1]
    tensor_size = lax.axis_size("tensor")
    count = tensor_size // 4
    each = rows // tensor_size
    group = lax.axis_index("groups").astype(jnp.int32)[None]
    place = lax.axis_index("tensor").astype(jnp.int32)[None]

    parts = local_rotation(group, gate_act, up_act)
    near = exchanged(parts, 0, 1)
    chunks = 4
    weights = [unpack(group, codes, scales, c, width // chunks) for c in range(chunks)]
    core = place[0] % 2
    parts = jnp.where(
        core == 0,
        parts.astype(jnp.float32) + near.astype(jnp.float32),
        near.astype(jnp.float32) - parts.astype(jnp.float32),
    ).astype(jnp.bfloat16)
    mine, theirs = parts[0], parts[1]
    across_y = exchanged(mine, 0, 2).astype(jnp.float32)
    across_x = exchanged(theirs, 1, 0).astype(jnp.float32)
    across_xy = exchanged(theirs, 1, 2).astype(jnp.float32)
    low = place[0] // 2 % 2 == 0
    here = mine.astype(jnp.float32)
    both = jnp.concatenate(
        [
            jnp.where(low, here + across_y, across_y - here),
            jnp.where(low, across_x + across_xy, across_xy - across_x),
        ]
    ).astype(jnp.bfloat16)
    others = [exchanged(both, 0, 4 * d) for d in range(1, count)]
    keep, send = product(place, both, others, weights)

    keep = keep + exchanged(send, 0, 1).astype(jnp.float32)
    quarters = keep.reshape(4, count * each, width)
    send = quarters[1:].astype(jnp.bfloat16)
    keep = (
        quarters[0]
        + exchanged(send[0], 0, 2).astype(jnp.float32)
        + exchanged(send[1], 1, 0).astype(jnp.float32)
        + exchanged(send[2], 1, 2).astype(jnp.float32)
    )
    send = keep.astype(jnp.bfloat16)
    total = keep[:each]
    for d in range(1, count):
        total = total + exchanged(send[d * each : (d + 1) * each], 0, 4 * d).astype(jnp.float32)
    return total.astype(jnp.bfloat16)


def body(gate_act, up_act, codes, scales):
    tensor_size = lax.axis_size("tensor")
    blocks = gate_act.shape[0] // HAD_LOCAL
    if (
        lax.axis_size("groups") == 2
        and tensor_size >= 4
        and blocks % 2 == 0
        and gate_act.shape[1] % tensor_size == 0
        and blocks * gate_act.shape[1] <= 128
    ):
        return shared_body(gate_act, up_act, codes, scales)
    return general_body(gate_act, up_act, codes, scales)


def solution(mesh):
    placed = (P("tensor", "groups"), P("tensor", "groups"), P("tensor", None), P("tensor", None))
    return jax.shard_map(
        body, mesh=mesh, in_specs=placed, out_specs=P(("groups", "tensor"), None), check_vma=False
    )
```

```python
import functools
import math

import jax
import jax.numpy as jnp
import numpy as np
from jax import lax
from jax.experimental import pallas as pl
from jax.experimental.pallas import tpu as pltpu
from jax.sharding import PartitionSpec as P

HAD_CROSS = 128
GROUP = 32
HAD_LOCAL = 416
PAIRS = HAD_LOCAL // 2
WORDS_PER_GROUP = GROUP // 2
AXES = ("groups", "tensor")
MIB = 2**20
TILE = 512
LANES = 128


def paley_table():
    squares = set()
    for real_part in range(5):
        for root_part in range(5):
            squares.add(
                (
                    (real_part * real_part + 2 * root_part * root_part) % 5,
                    2 * real_part * root_part % 5,
                )
            )
    jacobsthal = np.zeros((25, 25))
    for first in range(25):
        for second in range(25):
            differ = ((first // 5 - second // 5) % 5, (first % 5 - second % 5) % 5)
            if differ == (0, 0):
                jacobsthal[first, second] = 0.0
            elif differ in squares:
                jacobsthal[first, second] = 1.0
            else:
                jacobsthal[first, second] = -1.0
    conference = np.zeros((26, 26))
    conference[0, 1:] = 1.0
    conference[1:, 0] = 1.0
    conference[1:, 1:] = jacobsthal
    return np.kron(conference, np.array([[1.0, 1.0], [1.0, -1.0]])) + np.kron(
        np.eye(26), np.array([[1.0, -1.0], [-1.0, -1.0]])
    )


def walsh_table(order):
    matrix = np.ones((1, 1))
    while matrix.shape[0] < order:
        matrix = np.kron(np.array([[1.0, 1.0], [1.0, -1.0]]), matrix)
    return matrix


def local_matrix(order):
    return np.kron(walsh_table(order // 52), paley_table()) / math.sqrt(order)


def hadamard_local(order):
    return jnp.asarray(local_matrix(order), dtype=jnp.float32).astype(jnp.bfloat16)


def sign_table(order):
    return jnp.asarray(walsh_table(order), dtype=jnp.float32)


def swapped(value, axis, distance):
    mask = 2**distance
    pairs = [(source, source ^ mask) for source in range(lax.axis_size(axis))]
    return lax.ppermute(value, axis, pairs)


def dequantize(words, group_scales):
    low_codes = words % 16
    high_codes = words // 16
    unpacked = jnp.stack([low_codes, high_codes], axis=1).reshape(
        2 * words.shape[0], words.shape[1]
    )
    spread = jnp.repeat(group_scales.astype(jnp.float32), GROUP, axis=0)
    return ((unpacked - 8).astype(jnp.float32) * spread).astype(jnp.bfloat16)


def general_body(gate_act, up_act, codes, scales):
    units_here = gate_act.shape[0]
    total_rows = gate_act.shape[1]
    blocks_here = units_here // HAD_LOCAL
    factor = 1.0 / math.sqrt(HAD_CROSS)
    hidden = (jax.nn.silu(gate_act.astype(jnp.float32)) * up_act.astype(jnp.float32)).astype(
        jnp.bfloat16
    )
    hidden = hidden.reshape(blocks_here, HAD_LOCAL, total_rows)
    local = jnp.einsum(
        "kn,anr->akr", hadamard_local(HAD_LOCAL), hidden, preferred_element_type=jnp.float32
    ).astype(jnp.bfloat16)
    partial_sums = jnp.einsum(
        "abr,ae->ebr",
        local.astype(jnp.float32),
        sign_table(blocks_here),
        precision=lax.Precision.HIGHEST,
    )
    my_index = lax.axis_index("tensor")
    for bit_pos in range(lax.axis_size("tensor").bit_length() - 1):
        partner = swapped(partial_sums, "tensor", bit_pos)
        upper = my_index // 2**bit_pos % 2
        partial_sums = jnp.where(upper == 0, partial_sums + partner, partner - partial_sums)
    rotated = (partial_sums * factor).astype(jnp.bfloat16)
    rotated = rotated.reshape(units_here, total_rows)
    weight = dequantize(codes, scales)
    summed = lax.psum_scatter(
        lax.dot_general(
            rotated, weight, (((0,), (0,)), ((), ())), preferred_element_type=jnp.float32
        ),
        "tensor",
        scatter_dimension=0,
        tiled=True,
    )
    return summed.astype(jnp.bfloat16)


def exchanged(value, group_mask, tensor_mask):
    tensor_size = lax.axis_size("tensor")
    pairs = [
        (g * tensor_size + t, (g ^ group_mask) * tensor_size + (t ^ tensor_mask))
        for g in range(lax.axis_size("groups"))
        for t in range(tensor_size)
    ]
    return lax.ppermute(value, AXES, pairs)


def in_hbm(array):
    return pltpu.with_memory_space_constraint(array, pltpu.HBM)


def parity_sign(bits, masks):
    total = jnp.int32(0)
    position = 1
    while position <= masks:
        if masks & position:
            total = total + bits // position % 2
        position *= 2
    return (1 - 2 * (total % 2)).astype(jnp.float32)


def local_kernel(
    group_ref, gate_hbm, up_hbm, table_hbm, out_ref, gate_in, up_in, table, hidden_sc, stack_sc, mix_sc, sems
):
    copies = [
        pltpu.make_async_copy(source, target, sems.at[index])
        for index, (source, target) in enumerate(
            ((gate_hbm, gate_in), (up_hbm, up_in), (table_hbm, table))
        )
    ]
    for copy in copies:
        copy.start()
    rows = gate_in.shape[0]
    blocks = gate_in.shape[1] // HAD_LOCAL
    half = blocks // 2
    line = lax.broadcasted_iota(jnp.int32, (blocks * rows, blocks * rows), 0)
    column = lax.broadcasted_iota(jnp.int32, (blocks * rows, blocks * rows), 1)
    common = (line // rows) & (column // rows)
    odd = jnp.zeros_like(common)
    for bit_pos in range(blocks.bit_length() - 1):
        odd = odd ^ ((common >> bit_pos) & 1)
    walsh = jnp.where(line % rows == column % rows, 1 - 2 * odd, 0)
    walsh = walsh.astype(jnp.float32).astype(jnp.bfloat16)
    copies[0].wait()
    copies[1].wait()
    gate = gate_in[...].astype(jnp.float32)
    hidden_sc[...] = gate / (1.0 + jnp.exp(-gate)) * up_in[...].astype(jnp.float32)
    for a in range(blocks):
        stack_sc[a * rows : (a + 1) * rows, :] = hidden_sc[
            :, a * HAD_LOCAL : (a + 1) * HAD_LOCAL
        ].astype(jnp.bfloat16)
    copies[2].wait()
    hidden = stack_sc[...]
    wide = table.shape[0] // HAD_LOCAL
    for piece in range(wide):
        local = jnp.dot(
            hidden,
            table[piece * HAD_LOCAL : (piece + 1) * HAD_LOCAL, :],
            preferred_element_type=jnp.float32,
        ).astype(jnp.bfloat16)
        mix_sc[:, piece * LANES : (piece + 1) * LANES] = jnp.dot(
            walsh, local, preferred_element_type=jnp.float32
        ).astype(jnp.bfloat16)
    padded = wide * LANES // 2
    group = group_ref[0]
    for part in range(2):
        first = (group if part == 0 else 1 - group) * half
        for parity in range(2):
            for e in range(half):
                start = pl.multiple_of((first + e) * rows, rows)
                offset = (parity * half + e) * PAIRS
                out_ref[part, :, offset : offset + PAIRS] = mix_sc[
                    pl.ds(start, rows), parity * padded : parity * padded + PAIRS
                ]


def local_rotation(group, gate_act, up_act):
    units, rows = gate_act.shape
    blocks = units // HAD_LOCAL
    padded = -(-PAIRS // LANES) * LANES
    by_parity = local_matrix(HAD_LOCAL).reshape(PAIRS, 2, HAD_LOCAL)
    table = np.zeros((HAD_LOCAL, 2 * padded), np.float32)
    table[:, :PAIRS] = by_parity[:, 0].T
    table[:, padded : padded + PAIRS] = by_parity[:, 1].T
    table = np.concatenate(np.split(table, 2 * padded // LANES, axis=1))
    hbm = pl.BlockSpec(memory_space=pltpu.HBM)
    return pl.pallas_call(
        local_kernel,
        in_specs=[pl.BlockSpec(memory_space=pltpu.SMEM), hbm, hbm, hbm],
        out_specs=pl.BlockSpec(memory_space=pltpu.VMEM),
        out_shape=jax.ShapeDtypeStruct((2, rows, units // 2), jnp.bfloat16),
        scratch_shapes=[
            pltpu.VMEM((rows, units), jnp.bfloat16),
            pltpu.VMEM((rows, units), jnp.bfloat16),
            pltpu.VMEM(table.shape, jnp.bfloat16),
            pltpu.VMEM((rows, units), jnp.float32),
            pltpu.VMEM((blocks * rows, HAD_LOCAL), jnp.bfloat16),
            pltpu.VMEM((blocks * rows, 2 * padded), jnp.bfloat16),
            pltpu.SemaphoreType.DMA((3,)),
        ],
        compiler_params=pltpu.CompilerParams(vmem_limit_bytes=10 * MIB),
        cost_estimate=pl.CostEstimate(flops=10**8, bytes_accessed=2 * MIB, transcendentals=10**5),
        name="local_rotation",
    )(group, in_hbm(gate_act.T), in_hbm(up_act.T), in_hbm(jnp.asarray(table, jnp.bfloat16)))


def unpack_span(words, scale):
    scale = jnp.broadcast_to(scale, words.shape).astype(jnp.bfloat16)
    eight = jnp.bfloat16(8)
    low = (words & 15).astype(jnp.float32).astype(jnp.bfloat16)
    high = (words >> 4).astype(jnp.float32).astype(jnp.bfloat16)
    return (low - eight) * scale, (high - eight) * scale


def unpack_kernel(tile, group_ref, codes_hbm, scales_hbm, out_ref, rest_ref, words, scales, wide, sems):
    count, rows, columns = words.shape
    spans = rows // WORDS_PER_GROUP
    per = count * spans
    plane = out_ref.shape[0] // 2
    group = group_ref[0]
    first = pltpu.make_async_copy(scales_hbm, scales, sems.at[count])
    first.start()
    copies = []
    for step in range(count):
        at = pl.multiple_of((group * count + step) * rows, rows)
        copies.append(
            pltpu.make_async_copy(
                codes_hbm.at[pl.ds(at, rows), pl.ds(0, columns)], words.at[step], sems.at[step]
            )
        )
        copies[-1].start()
    first.wait()
    wide[...] = scales[...].astype(jnp.float32)
    rest_ref[...] = jnp.where(group == 0, wide[:per, columns:], wide[per:, columns:])
    for step in range(count):
        copies[step].wait()

        @pl.loop(0, columns // tile)
        def _(i, step=step):
            here = pl.ds(pl.multiple_of(i * tile, tile), tile)
            for p in range(spans):
                top = p * WORDS_PER_GROUP
                low, high = unpack_span(
                    words[step, top : top + WORDS_PER_GROUP, here],
                    wide[pl.ds(group * per + step * spans + p, 1), here],
                )
                at = step * rows + top
                out_ref[at : at + WORDS_PER_GROUP, here] = low
                out_ref[plane + at : plane + at + WORDS_PER_GROUP, here] = high


def unpack(group, codes, scales, columns, tile):
    words, width = codes.shape
    half = words // 2
    hbm = pl.BlockSpec(memory_space=pltpu.HBM)
    vmem = pl.BlockSpec(memory_space=pltpu.VMEM)
    count = half // PAIRS
    per = half // WORDS_PER_GROUP
    return pl.pallas_call(
        functools.partial(unpack_kernel, tile),
        in_specs=[pl.BlockSpec(memory_space=pltpu.SMEM), hbm, hbm],
        out_specs=[vmem, vmem],
        out_shape=[
            pltpu.VMEM((words, columns), jnp.bfloat16),
            pltpu.VMEM((per, width - columns), jnp.float32),
        ],
        scratch_shapes=[
            pltpu.VMEM((count, PAIRS, columns), jnp.int32),
            pltpu.VMEM(scales.shape, jnp.bfloat16),
            pltpu.VMEM(scales.shape, jnp.float32),
            pltpu.SemaphoreType.DMA((count + 1,)),
        ],
        compiler_params=pltpu.CompilerParams(vmem_limit_bytes=24 * MIB),
        cost_estimate=pl.CostEstimate(
            flops=words * columns * 8, bytes_accessed=words * columns * 4, transcendentals=0
        ),
        name="unpack",
    )(group, in_hbm(codes), in_hbm(scales))


def product_kernel(
    tile, place_ref, codes_hbm, own_ref, *refs
):
    *others, ready_ref, scales_ref, keep_ref, send_ref, words, first_sc, second_sc, sems = refs
    rows = own_ref.shape[0]
    group, place = place_ref[0], place_ref[1]
    height = words.shape[1]
    base = ready_ref.shape[1]
    loops = scales_ref.shape[1] // tile
    line = pl.multiple_of(group * height, height)

    def fetch(index, slot):
        at = pl.multiple_of(base + index * tile, tile)
        return pltpu.make_async_copy(
            codes_hbm.at[pl.ds(line, height), pl.ds(at, tile)], words.at[slot], sems.at[slot]
        )

    fetch(0, 0).start()
    fetch(1, 1).start()

    count = len(others) + 1
    far = 4 * (count - 1)
    total = own_ref[...].astype(jnp.float32) * parity_sign(place, far)
    for index, other in enumerate(others):
        total = total + other[...].astype(jnp.float32) * parity_sign(
            place & (place ^ (4 * (index + 1))), far
        )
    rotated = (total * (1.0 / math.sqrt(HAD_CROSS))).astype(jnp.bfloat16)
    each = rows // (8 * count)
    slot = lax.broadcasted_iota(jnp.int32, (rows, rows), 0)
    column = lax.broadcasted_iota(jnp.int32, (rows, rows), 1)
    unit = slot // each
    away = unit // (4 * count) + 2 * (unit // count % 2) + 4 * (unit % count)
    source = (unit // (2 * count) % 2) * (rows // 2) + (away ^ place) * each + slot % each
    pick = (column == source).astype(jnp.float32).astype(jnp.bfloat16)
    rotated = jnp.dot(pick, rotated, preferred_element_type=jnp.float32).astype(jnp.bfloat16)

    def multiply(weight, at):
        result = jnp.dot(rotated, weight, preferred_element_type=jnp.float32)
        to = pl.ds(pl.multiple_of(at, tile), tile)
        keep_ref[:, to] = result[: rows // 2]
        send_ref[:, to] = result[rows // 2 :].astype(jnp.bfloat16)

    def unpack_tile(index, slot, target):
        here = pl.ds(pl.multiple_of(index * tile, tile), tile)
        for p in range(height // WORDS_PER_GROUP):
            top = p * WORDS_PER_GROUP
            low, high = unpack_span(
                words[slot, top : top + WORDS_PER_GROUP, :], scales_ref[p : p + 1, here]
            )
            target[top : top + WORDS_PER_GROUP, :] = low
            target[height + top : height + top + WORDS_PER_GROUP, :] = high

    def stage(index, slot, target, previous):
        fetch(index, slot).wait()
        ready = pl.ds(pl.multiple_of(index * tile, tile), tile)
        multiply(ready_ref[:, ready], index * tile)
        if previous is not None:
            multiply(previous[...], base + (index - 1) * tile)
        unpack_tile(index, slot, target)

    stage(0, 0, first_sc, None)
    fetch(2, 0).start()

    @pl.loop(0, loops // 2 - 1)
    def _(i):
        stage(2 * i + 1, 1, second_sc, first_sc)
        fetch(2 * i + 3, 1).start()
        stage(2 * i + 2, 0, first_sc, second_sc)

        @pl.when(2 * i + 4 < loops)
        def _():
            fetch(2 * i + 4, 0).start()

    stage(loops - 1, 1, second_sc, first_sc)
    multiply(second_sc[...], base + (loops - 1) * tile)


def product(place, codes, own, others, ready, scales, tile):
    rows = own.shape[0]
    words, width = codes.shape
    hbm = pl.BlockSpec(memory_space=pltpu.HBM)
    vmem = pl.BlockSpec(memory_space=pltpu.VMEM)
    return pl.pallas_call(
        functools.partial(product_kernel, tile),
        in_specs=[pl.BlockSpec(memory_space=pltpu.SMEM), hbm] + [vmem] * (3 + len(others)),
        out_specs=[vmem, vmem],
        out_shape=[
            jax.ShapeDtypeStruct((rows // 2, width), jnp.float32),
            jax.ShapeDtypeStruct((rows // 2, width), jnp.bfloat16),
        ],
        scratch_shapes=[
            pltpu.VMEM((2, words // 2, tile), jnp.int32),
            pltpu.VMEM((words, tile), jnp.bfloat16),
            pltpu.VMEM((words, tile), jnp.bfloat16),
            pltpu.SemaphoreType.DMA((2,)),
        ],
        compiler_params=pltpu.CompilerParams(vmem_limit_bytes=16 * MIB),
        name="product",
    )(
        place,
        in_hbm(codes),
        own,
        *others,
        pltpu.with_memory_space_constraint(ready, pltpu.VMEM),
        pltpu.with_memory_space_constraint(scales, pltpu.VMEM),
    )


def shared_body(gate_act, up_act, codes, scales):
    rows = gate_act.shape[1]
    width = codes.shape[1]
    tensor_size = lax.axis_size("tensor")
    count = tensor_size // 4
    each = rows // tensor_size
    group = lax.axis_index("groups").astype(jnp.int32)[None]
    place = lax.axis_index("tensor").astype(jnp.int32)[None]

    parts = local_rotation(group, gate_act, up_act)
    near = exchanged(parts, 0, 1)
    core = place[0] % 2
    parts = jnp.where(
        core == 0,
        parts.astype(jnp.float32) + near.astype(jnp.float32),
        near.astype(jnp.float32) - parts.astype(jnp.float32),
    ).astype(jnp.bfloat16)
    mine, theirs = parts[0], parts[1]
    across_y = exchanged(mine, 0, 2).astype(jnp.float32)
    across_x = exchanged(theirs, 1, 0).astype(jnp.float32)
    across_xy = exchanged(theirs, 1, 2).astype(jnp.float32)
    low = place[0] // 2 % 2 == 0
    here = mine.astype(jnp.float32)
    both = jnp.concatenate(
        [
            jnp.where(low, here + across_y, across_y - here),
            jnp.where(low, across_x + across_xy, across_xy - across_x),
        ]
    ).astype(jnp.bfloat16)
    both, group_then = lax.optimization_barrier((both, group))
    others = [exchanged(both, 0, 4 * d) for d in range(1, count)]
    ready, rest = unpack(group_then, codes, scales, width // 2, TILE)
    keep, send = product(
        jnp.concatenate([group, place]), codes, both, others, ready, rest, TILE
    )

    keep = keep + exchanged(send, 0, 1).astype(jnp.float32)
    quarters = keep.reshape(4, count * each, width)
    send = quarters[1:].astype(jnp.bfloat16)
    keep = (
        quarters[0]
        + exchanged(send[0], 0, 2).astype(jnp.float32)
        + exchanged(send[1], 1, 0).astype(jnp.float32)
        + exchanged(send[2], 1, 2).astype(jnp.float32)
    )
    while keep.shape[0] > each:
        half = keep.shape[0] // 2
        send = keep[half:].astype(jnp.bfloat16)
        keep = keep[:half] + exchanged(send, 0, 4 * half // each).astype(jnp.float32)
    return keep.astype(jnp.bfloat16)


def body(gate_act, up_act, codes, scales):
    tensor_size = lax.axis_size("tensor")
    blocks = gate_act.shape[0] // HAD_LOCAL
    if (
        lax.axis_size("groups") == 2
        and tensor_size >= 4
        and blocks % 2 == 0
        and gate_act.shape[1] % tensor_size == 0
        and blocks * gate_act.shape[1] <= 128
        and codes.shape[1] % (4 * TILE) == 0
    ):
        return shared_body(gate_act, up_act, codes, scales)
    return general_body(gate_act, up_act, codes, scales)


def solution(mesh):
    placed = (P("tensor", "groups"), P("tensor", "groups"), P("tensor", None), P("tensor", None))
    return jax.shard_map(
        body, mesh=mesh, in_specs=placed, out_specs=P(("groups", "tensor"), None), check_vma=False
    )
```

```python
import functools
import math

import jax
import jax.numpy as jnp
import numpy as np
from jax import lax
from jax.experimental import pallas as pl
from jax.experimental.pallas import tpu as pltpu
from jax.sharding import PartitionSpec as P

HAD_CROSS = 128
GROUP = 32
HAD_LOCAL = 416
PAIRS = HAD_LOCAL // 2
WORDS_PER_GROUP = GROUP // 2
AXES = ("groups", "tensor")
MIB = 2**20
TILE = 512
CHUNK = 256
FETCHES = (3, 5, 4)
LANES = 128


def paley_table():
    squares = set()
    for real_part in range(5):
        for root_part in range(5):
            squares.add(
                (
                    (real_part * real_part + 2 * root_part * root_part) % 5,
                    2 * real_part * root_part % 5,
                )
            )
    jacobsthal = np.zeros((25, 25))
    for first in range(25):
        for second in range(25):
            differ = ((first // 5 - second // 5) % 5, (first % 5 - second % 5) % 5)
            if differ == (0, 0):
                jacobsthal[first, second] = 0.0
            elif differ in squares:
                jacobsthal[first, second] = 1.0
            else:
                jacobsthal[first, second] = -1.0
    conference = np.zeros((26, 26))
    conference[0, 1:] = 1.0
    conference[1:, 0] = 1.0
    conference[1:, 1:] = jacobsthal
    return np.kron(conference, np.array([[1.0, 1.0], [1.0, -1.0]])) + np.kron(
        np.eye(26), np.array([[1.0, -1.0], [-1.0, -1.0]])
    )


def walsh_table(order):
    matrix = np.ones((1, 1))
    while matrix.shape[0] < order:
        matrix = np.kron(np.array([[1.0, 1.0], [1.0, -1.0]]), matrix)
    return matrix


def local_matrix(order):
    return np.kron(walsh_table(order // 52), paley_table()) / math.sqrt(order)


def hadamard_local(order):
    return jnp.asarray(local_matrix(order), dtype=jnp.float32).astype(jnp.bfloat16)


def sign_table(order):
    return jnp.asarray(walsh_table(order), dtype=jnp.float32)


def swapped(value, axis, distance):
    mask = 2**distance
    pairs = [(source, source ^ mask) for source in range(lax.axis_size(axis))]
    return lax.ppermute(value, axis, pairs)


def dequantize(words, group_scales):
    low_codes = words % 16
    high_codes = words // 16
    unpacked = jnp.stack([low_codes, high_codes], axis=1).reshape(
        2 * words.shape[0], words.shape[1]
    )
    spread = jnp.repeat(group_scales.astype(jnp.float32), GROUP, axis=0)
    return ((unpacked - 8).astype(jnp.float32) * spread).astype(jnp.bfloat16)


def general_body(gate_act, up_act, codes, scales):
    units_here = gate_act.shape[0]
    total_rows = gate_act.shape[1]
    blocks_here = units_here // HAD_LOCAL
    factor = 1.0 / math.sqrt(HAD_CROSS)
    hidden = (jax.nn.silu(gate_act.astype(jnp.float32)) * up_act.astype(jnp.float32)).astype(
        jnp.bfloat16
    )
    hidden = hidden.reshape(blocks_here, HAD_LOCAL, total_rows)
    local = jnp.einsum(
        "kn,anr->akr", hadamard_local(HAD_LOCAL), hidden, preferred_element_type=jnp.float32
    ).astype(jnp.bfloat16)
    partial_sums = jnp.einsum(
        "abr,ae->ebr",
        local.astype(jnp.float32),
        sign_table(blocks_here),
        precision=lax.Precision.HIGHEST,
    )
    my_index = lax.axis_index("tensor")
    for bit_pos in range(lax.axis_size("tensor").bit_length() - 1):
        partner = swapped(partial_sums, "tensor", bit_pos)
        upper = my_index // 2**bit_pos % 2
        partial_sums = jnp.where(upper == 0, partial_sums + partner, partner - partial_sums)
    rotated = (partial_sums * factor).astype(jnp.bfloat16)
    rotated = rotated.reshape(units_here, total_rows)
    weight = dequantize(codes, scales)
    summed = lax.psum_scatter(
        lax.dot_general(
            rotated, weight, (((0,), (0,)), ((), ())), preferred_element_type=jnp.float32
        ),
        "tensor",
        scatter_dimension=0,
        tiled=True,
    )
    return summed.astype(jnp.bfloat16)


def exchanged(value, group_mask, tensor_mask):
    tensor_size = lax.axis_size("tensor")
    pairs = [
        (g * tensor_size + t, (g ^ group_mask) * tensor_size + (t ^ tensor_mask))
        for g in range(lax.axis_size("groups"))
        for t in range(tensor_size)
    ]
    return lax.ppermute(value, AXES, pairs)


def in_hbm(array):
    return pltpu.with_memory_space_constraint(array, pltpu.HBM)


def parity_sign(bits, masks):
    total = jnp.int32(0)
    position = 1
    while position <= masks:
        if masks & position:
            total = total + bits // position % 2
        position *= 2
    return (1 - 2 * (total % 2)).astype(jnp.float32)


def fetches(codes_hbm, group, first, count, words, sems, sem):
    height, tile = words.shape[1:]
    line = pl.multiple_of(group * height, height)
    return [
        pltpu.make_async_copy(
            codes_hbm.at[pl.ds(line, height), pl.ds((first + i) * tile, tile)],
            words.at[i],
            sems.at[sem + i],
        )
        for i in range(count)
    ]


def local_kernel(
    group_ref,
    gate_hbm,
    up_hbm,
    table_hbm,
    out_ref,
    gate_in,
    up_in,
    table,
    hidden_sc,
    stack_sc,
    mix_sc,
    sems,
):
    group = group_ref[0]
    copies = [
        pltpu.make_async_copy(source, target, sems.at[index])
        for index, (source, target) in enumerate(
            ((gate_hbm, gate_in), (up_hbm, up_in), (table_hbm, table))
        )
    ]
    for copy in copies:
        copy.start()
    rows = gate_in.shape[0]
    blocks = gate_in.shape[1] // HAD_LOCAL
    half = blocks // 2
    line = lax.broadcasted_iota(jnp.int32, (blocks * rows, blocks * rows), 0)
    column = lax.broadcasted_iota(jnp.int32, (blocks * rows, blocks * rows), 1)
    common = (line // rows) & (column // rows)
    odd = jnp.zeros_like(common)
    for bit_pos in range(blocks.bit_length() - 1):
        odd = odd ^ ((common >> bit_pos) & 1)
    walsh = jnp.where(line % rows == column % rows, 1 - 2 * odd, 0)
    walsh = walsh.astype(jnp.float32).astype(jnp.bfloat16)
    copies[0].wait()
    copies[1].wait()
    gate = gate_in[...].astype(jnp.float32)
    hidden_sc[...] = gate / (1.0 + jnp.exp(-gate)) * up_in[...].astype(jnp.float32)
    for a in range(blocks):
        stack_sc[a * rows : (a + 1) * rows, :] = hidden_sc[
            :, a * HAD_LOCAL : (a + 1) * HAD_LOCAL
        ].astype(jnp.bfloat16)
    copies[2].wait()
    hidden = stack_sc[...]
    wide = table.shape[0] // HAD_LOCAL
    for piece in range(wide):
        local = jnp.dot(
            hidden,
            table[piece * HAD_LOCAL : (piece + 1) * HAD_LOCAL, :],
            preferred_element_type=jnp.float32,
        ).astype(jnp.bfloat16)
        mix_sc[:, piece * LANES : (piece + 1) * LANES] = jnp.dot(
            walsh, local, preferred_element_type=jnp.float32
        ).astype(jnp.bfloat16)
    padded = wide * LANES // 2
    for part in range(2):
        first = (group if part == 0 else 1 - group) * half
        for parity in range(2):
            for e in range(half):
                start = pl.multiple_of((first + e) * rows, rows)
                offset = (parity * half + e) * PAIRS
                out_ref[part, :, offset : offset + PAIRS] = mix_sc[
                    pl.ds(start, rows), parity * padded : parity * padded + PAIRS
                ]


def local_rotation(group, gate_act, up_act):
    units, rows = gate_act.shape
    blocks = units // HAD_LOCAL
    padded = -(-PAIRS // LANES) * LANES
    by_parity = local_matrix(HAD_LOCAL).reshape(PAIRS, 2, HAD_LOCAL)
    table = np.zeros((HAD_LOCAL, 2 * padded), np.float32)
    table[:, :PAIRS] = by_parity[:, 0].T
    table[:, padded : padded + PAIRS] = by_parity[:, 1].T
    table = np.concatenate(np.split(table, 2 * padded // LANES, axis=1))
    hbm = pl.BlockSpec(memory_space=pltpu.HBM)
    vmem = pl.BlockSpec(memory_space=pltpu.VMEM)
    return pl.pallas_call(
        local_kernel,
        in_specs=[pl.BlockSpec(memory_space=pltpu.SMEM)] + [hbm] * 3,
        out_specs=vmem,
        out_shape=jax.ShapeDtypeStruct((2, rows, units // 2), jnp.bfloat16),
        scratch_shapes=[
            pltpu.VMEM((rows, units), jnp.bfloat16),
            pltpu.VMEM((rows, units), jnp.bfloat16),
            pltpu.VMEM(table.shape, jnp.bfloat16),
            pltpu.VMEM((rows, units), jnp.float32),
            pltpu.VMEM((blocks * rows, HAD_LOCAL), jnp.bfloat16),
            pltpu.VMEM((blocks * rows, 2 * padded), jnp.bfloat16),
            pltpu.SemaphoreType.DMA((3,)),
        ],
        compiler_params=pltpu.CompilerParams(vmem_limit_bytes=6 * MIB),
        cost_estimate=pl.CostEstimate(flops=10**8, bytes_accessed=8 * MIB, transcendentals=10**5),
        name="local_rotation",
    )(
        group,
        in_hbm(gate_act.T),
        in_hbm(up_act.T),
        in_hbm(jnp.asarray(table, jnp.bfloat16)),
    )


def unpack_span(words, scale):
    scale = jnp.broadcast_to(scale, words.shape).astype(jnp.bfloat16)
    eight = jnp.bfloat16(8)
    low = (words & 15).astype(jnp.float32).astype(jnp.bfloat16)
    high = (words >> 4).astype(jnp.float32).astype(jnp.bfloat16)
    return (low - eight) * scale, (high - eight) * scale


def widen(group, scales_ref, wide_ref):
    per = wide_ref.shape[0]
    for part in range(2):

        @pl.when(group == part)
        def _(part=part):
            wide_ref[...] = scales_ref[part * per : (part + 1) * per, :].astype(jnp.float32)


def unpack_tile(words, scales_ref, column, target, at, spans):
    height, tile = words.shape
    for p in spans:
        top = p * WORDS_PER_GROUP
        low, high = unpack_span(
            words[top : top + WORDS_PER_GROUP, :], scales_ref[p : p + 1, pl.ds(column, tile)]
        )
        target[top : top + WORDS_PER_GROUP, pl.ds(at, tile)] = low
        target[height + top : height + top + WORDS_PER_GROUP, pl.ds(at, tile)] = high


def fetch_kernel(group_ref, codes_hbm, scales_hbm, next_ref, wide_ref, scales, sems):
    ahead = next_ref.shape[0]
    arrival = pltpu.make_async_copy(scales_hbm, scales, sems.at[ahead])
    arrival.start()
    copies = fetches(codes_hbm, group_ref[0], 0, ahead, next_ref, sems, 0)
    for copy in copies:
        copy.start()
    arrival.wait()
    widen(group_ref[0], scales, wide_ref)
    for copy in copies:
        copy.wait()


def fetch(group, codes, scales, ahead):
    words, width = codes.shape
    hbm = pl.BlockSpec(memory_space=pltpu.HBM)
    vmem = pl.BlockSpec(memory_space=pltpu.VMEM)
    return pl.pallas_call(
        fetch_kernel,
        in_specs=[pl.BlockSpec(memory_space=pltpu.SMEM), hbm, hbm],
        out_specs=[vmem, vmem],
        out_shape=[
            pltpu.VMEM((ahead, words // 2, TILE), codes.dtype),
            pltpu.VMEM((words // 2 // WORDS_PER_GROUP, width), jnp.float32),
        ],
        scratch_shapes=[
            pltpu.VMEM(scales.shape, scales.dtype),
            pltpu.SemaphoreType.DMA((ahead + 1,)),
        ],
        compiler_params=pltpu.CompilerParams(vmem_limit_bytes=4 * MIB),
        cost_estimate=pl.CostEstimate(
            flops=0, bytes_accessed=ahead * words * TILE * 2, transcendentals=0
        ),
        name="fetch",
    )(group, in_hbm(codes), in_hbm(scales))


def unpack_kernel(group_ref, codes_hbm, scales_ref, given, out_ref, next_ref, words, sems):
    group = group_ref[0]
    count, height, tile = given.shape
    own, ahead = words.shape[0], next_ref.shape[0]
    copies = fetches(codes_hbm, group, count, own, words, sems, 0)
    copies += fetches(codes_hbm, group, count + own, ahead, next_ref, sems, own)
    for copy in copies:
        copy.start()
    spans = range(height // WORDS_PER_GROUP)

    @pl.loop(0, count)
    def _(i):
        at = pl.multiple_of(i * tile, tile)
        unpack_tile(given.at[i], scales_ref, at, out_ref, at, spans)

    @pl.loop(0, own)
    def _(i):
        pltpu.make_async_copy(
            codes_hbm.at[pl.ds(0, height), pl.ds(0, tile)], words.at[i], sems.at[i]
        ).wait()
        at = pl.multiple_of((count + i) * tile, tile)
        unpack_tile(words.at[i], scales_ref, at, out_ref, at, spans)

    for copy in copies[own:]:
        copy.wait()


def unpack(group, codes, scales, given, own, ahead):
    words = codes.shape[0]
    hbm = pl.BlockSpec(memory_space=pltpu.HBM)
    vmem = pl.BlockSpec(memory_space=pltpu.VMEM)
    columns = (given.shape[0] + own) * TILE
    return pl.pallas_call(
        unpack_kernel,
        in_specs=[pl.BlockSpec(memory_space=pltpu.SMEM), hbm, vmem, vmem],
        out_specs=[vmem, vmem],
        out_shape=[
            pltpu.VMEM((words, columns), jnp.bfloat16),
            pltpu.VMEM((ahead, words // 2, TILE), codes.dtype),
        ],
        scratch_shapes=[
            pltpu.VMEM((own, words // 2, TILE), codes.dtype),
            pltpu.SemaphoreType.DMA((own + ahead,)),
        ],
        compiler_params=pltpu.CompilerParams(vmem_limit_bytes=(2 + 2 * own) * MIB),
        cost_estimate=pl.CostEstimate(
            flops=words * columns * 8, bytes_accessed=words * columns * 4, transcendentals=0
        ),
        name="unpack",
    )(
        group,
        in_hbm(codes),
        pltpu.with_memory_space_constraint(scales, pltpu.VMEM),
        pltpu.with_memory_space_constraint(given, pltpu.VMEM),
    )


def product_kernel(readies, place_ref, codes_hbm, given, scales_ref, own_ref, *refs):
    *others, keep_ref, send_ref, first_sc, second_sc, words, sems = refs
    ready_refs, others = others[:readies], others[readies:]
    rows = own_ref.shape[0]
    group, place = place_ref[0], place_ref[1]
    held, height, tile = given.shape
    ready_tiles = [
        (ref, i * tile) for ref in ready_refs for i in range(ref.shape[1] // tile)
    ]
    tiles = scales_ref.shape[1] // tile
    base = len(ready_tiles)
    own = tiles - base - held
    copies = fetches(codes_hbm, group, base + held, own, words, sems, 0)
    for copy in copies:
        copy.start()

    count = len(others) + 1
    far = 4 * (count - 1)
    total = own_ref[...].astype(jnp.float32) * parity_sign(place, far)
    for index, other in enumerate(others):
        total = total + other[...].astype(jnp.float32) * parity_sign(
            place & (place ^ (4 * (count - 1 - index))), far
        )
    rotated = (total * (1.0 / math.sqrt(HAD_CROSS))).astype(jnp.bfloat16)
    each = rows // (8 * count)
    slot = lax.broadcasted_iota(jnp.int32, (rows, rows), 0)
    column = lax.broadcasted_iota(jnp.int32, (rows, rows), 1)
    unit = slot // each
    away = unit // (4 * count) + 2 * (unit // count % 2) + 4 * (unit % count)
    source = (unit // (2 * count) % 2) * (rows // 2) + (away ^ place) * each + slot % each
    pick = (column == source).astype(jnp.float32).astype(jnp.bfloat16)
    rotated = jnp.dot(pick, rotated, preferred_element_type=jnp.float32).astype(jnp.bfloat16)

    depth = rotated.shape[1]
    spans = height // WORDS_PER_GROUP
    cuts = list(range(0, depth, CHUNK)) + [depth]

    def stage(products, fresh):
        sums = [None] * len(products)
        done = 0
        for k, (low, high) in enumerate(zip(cuts[:-1], cuts[1:])):
            for index, (weight, at, _) in enumerate(products):
                part = jnp.dot(
                    rotated[:, low:high],
                    weight[low:high, at : at + tile],
                    preferred_element_type=jnp.float32,
                )
                sums[index] = sums[index] + part if k else part
            if fresh is not None:
                source, column, target = fresh
                upto = spans * (k + 1) // (len(cuts) - 1)
                unpack_tile(source, scales_ref, column, target, 0, range(done, upto))
                done = upto
        for total, (_, _, to) in zip(sums, products):
            keep_ref[:, to : to + tile] = total[: rows // 2]
            send_ref[:, to : to + tile] = total[rows // 2 :].astype(jnp.bfloat16)

    waiting = [(ref, at, index * tile) for index, (ref, at) in enumerate(ready_tiles)]
    each_stage = -(-base // (tiles - base))
    previous = None
    for index in range(base, tiles):
        number = index - base
        if number >= held:
            copies[number - held].wait()
        source = given.at[number] if number < held else words.at[number - held]
        target = second_sc if number % 2 else first_sc
        products = waiting[:each_stage]
        waiting = waiting[each_stage:]
        if previous is not None:
            products.append(previous)
        stage(products, (source, index * tile, target))
        previous = (target, 0, index * tile)
    stage(waiting + [previous], None)


def product(place, codes, given, scales, own, others, ready):
    rows = own.shape[0]
    words, width = codes.shape
    hbm = pl.BlockSpec(memory_space=pltpu.HBM)
    vmem = pl.BlockSpec(memory_space=pltpu.VMEM)
    left = width // TILE - given.shape[0] - sum(r.shape[1] for r in ready) // TILE
    held = [pltpu.with_memory_space_constraint(r, pltpu.VMEM) for r in (given, scales)]
    return pl.pallas_call(
        functools.partial(product_kernel, len(ready)),
        in_specs=[pl.BlockSpec(memory_space=pltpu.SMEM), hbm]
        + [vmem] * (3 + len(ready) + len(others)),
        out_specs=[vmem, vmem],
        out_shape=[
            jax.ShapeDtypeStruct((rows // 2, width), jnp.float32),
            jax.ShapeDtypeStruct((rows // 2, width), jnp.bfloat16),
        ],
        scratch_shapes=[
            pltpu.VMEM((words, TILE), jnp.bfloat16),
            pltpu.VMEM((words, TILE), jnp.bfloat16),
            pltpu.VMEM((max(left, 1), words // 2, TILE), codes.dtype),
            pltpu.SemaphoreType.DMA((max(left, 1),)),
        ],
        compiler_params=pltpu.CompilerParams(vmem_limit_bytes=(8 + 2 * left) * MIB),
        name="product",
    )(
        place,
        in_hbm(codes),
        *held,
        own,
        *[pltpu.with_memory_space_constraint(r, pltpu.VMEM) for r in ready],
        *others,
    )


def shared_body(gate_act, up_act, codes, scales):
    rows = gate_act.shape[1]
    width = codes.shape[1]
    tensor_size = lax.axis_size("tensor")
    count = tensor_size // 4
    each = rows // tensor_size
    group = lax.axis_index("groups").astype(jnp.int32)[None]
    place = lax.axis_index("tensor").astype(jnp.int32)[None]

    tiles = width // TILE
    at_near, at_far, for_product = (tiles * n // 16 for n in FETCHES)
    parts = local_rotation(group, gate_act, up_act)
    near = exchanged(parts, 0, 1)
    core = place[0] % 2
    parts = jnp.where(
        core == 0,
        parts.astype(jnp.float32) + near.astype(jnp.float32),
        near.astype(jnp.float32) - parts.astype(jnp.float32),
    ).astype(jnp.bfloat16)
    parts, group_then = lax.optimization_barrier((parts, group))
    mine, theirs = parts[0], parts[1]
    across_y = exchanged(mine, 0, 2).astype(jnp.float32)
    across_x = exchanged(theirs, 1, 0).astype(jnp.float32)
    across_xy = exchanged(theirs, 1, 2).astype(jnp.float32)
    words, scales = fetch(group_then, codes, scales, at_near)
    low = place[0] // 2 % 2 == 0
    here = mine.astype(jnp.float32)
    both = jnp.concatenate(
        [
            jnp.where(low, here + across_y, across_y - here),
            jnp.where(low, across_x + across_xy, across_xy - across_x),
        ]
    ).astype(jnp.bfloat16)
    both, group_then, words = lax.optimization_barrier((both, group, words))
    others = [exchanged(both, 0, 4 * d) for d in range(count - 1, 0, -1)]
    ready, words = unpack(group_then, codes, scales, words, at_far, for_product)
    keep, send = product(
        jnp.concatenate([group, place]), codes, words, scales, both, others, [ready]
    )

    keep = keep + exchanged(send, 0, 1).astype(jnp.float32)
    quarters = keep.reshape(4, count * each, width)
    send = quarters[1:].astype(jnp.bfloat16)
    keep = (
        quarters[0]
        + exchanged(send[0], 0, 2).astype(jnp.float32)
        + exchanged(send[1], 1, 0).astype(jnp.float32)
        + exchanged(send[2], 1, 2).astype(jnp.float32)
    )
    while keep.shape[0] > each:
        half = keep.shape[0] // 2
        send = keep[half:].astype(jnp.bfloat16)
        keep = keep[:half] + exchanged(send, 0, 4 * half // each).astype(jnp.float32)
    return keep.astype(jnp.bfloat16)


def body(gate_act, up_act, codes, scales):
    tensor_size = lax.axis_size("tensor")
    blocks = gate_act.shape[0] // HAD_LOCAL
    if (
        lax.axis_size("groups") == 2
        and tensor_size >= 4
        and blocks % 2 == 0
        and gate_act.shape[1] % tensor_size == 0
        and blocks * gate_act.shape[1] <= 128
        and codes.shape[1] % (16 * TILE) == 0
    ):
        return shared_body(gate_act, up_act, codes, scales)
    return general_body(gate_act, up_act, codes, scales)


def solution(mesh):
    placed = (P("tensor", "groups"), P("tensor", "groups"), P("tensor", None), P("tensor", None))
    return jax.shard_map(
        body, mesh=mesh, in_specs=placed, out_specs=P(("groups", "tensor"), None), check_vma=False
    )
```

```python
import functools
import math

import jax
import jax.numpy as jnp
import numpy as np
from jax import lax
from jax.experimental import pallas as pl
from jax.experimental.pallas import tpu as pltpu
from jax.sharding import PartitionSpec as P

HAD_CROSS = 128
GROUP = 32
HAD_LOCAL = 416
PAIRS = HAD_LOCAL // 2
WORDS_PER_GROUP = GROUP // 2
AXES = ("groups", "tensor")
MIB = 2**20
TILE = 512
CHUNK = 256
FETCHES = (1, 2, 7, 3)
LANES = 128


def paley_table():
    squares = set()
    for real_part in range(5):
        for root_part in range(5):
            squares.add(
                (
                    (real_part * real_part + 2 * root_part * root_part) % 5,
                    2 * real_part * root_part % 5,
                )
            )
    jacobsthal = np.zeros((25, 25))
    for first in range(25):
        for second in range(25):
            differ = ((first // 5 - second // 5) % 5, (first % 5 - second % 5) % 5)
            if differ == (0, 0):
                jacobsthal[first, second] = 0.0
            elif differ in squares:
                jacobsthal[first, second] = 1.0
            else:
                jacobsthal[first, second] = -1.0
    conference = np.zeros((26, 26))
    conference[0, 1:] = 1.0
    conference[1:, 0] = 1.0
    conference[1:, 1:] = jacobsthal
    return np.kron(conference, np.array([[1.0, 1.0], [1.0, -1.0]])) + np.kron(
        np.eye(26), np.array([[1.0, -1.0], [-1.0, -1.0]])
    )


def walsh_table(order):
    matrix = np.ones((1, 1))
    while matrix.shape[0] < order:
        matrix = np.kron(np.array([[1.0, 1.0], [1.0, -1.0]]), matrix)
    return matrix


def local_matrix(order):
    return np.kron(walsh_table(order // 52), paley_table()) / math.sqrt(order)


def hadamard_local(order):
    return jnp.asarray(local_matrix(order), dtype=jnp.float32).astype(jnp.bfloat16)


def sign_table(order):
    return jnp.asarray(walsh_table(order), dtype=jnp.float32)


def swapped(value, axis, distance):
    mask = 2**distance
    pairs = [(source, source ^ mask) for source in range(lax.axis_size(axis))]
    return lax.ppermute(value, axis, pairs)


def dequantize(words, group_scales):
    low_codes = words % 16
    high_codes = words // 16
    unpacked = jnp.stack([low_codes, high_codes], axis=1).reshape(
        2 * words.shape[0], words.shape[1]
    )
    spread = jnp.repeat(group_scales.astype(jnp.float32), GROUP, axis=0)
    return ((unpacked - 8).astype(jnp.float32) * spread).astype(jnp.bfloat16)


def general_body(gate_act, up_act, codes, scales):
    units_here = gate_act.shape[0]
    total_rows = gate_act.shape[1]
    blocks_here = units_here // HAD_LOCAL
    factor = 1.0 / math.sqrt(HAD_CROSS)
    hidden = (jax.nn.silu(gate_act.astype(jnp.float32)) * up_act.astype(jnp.float32)).astype(
        jnp.bfloat16
    )
    hidden = hidden.reshape(blocks_here, HAD_LOCAL, total_rows)
    local = jnp.einsum(
        "kn,anr->akr", hadamard_local(HAD_LOCAL), hidden, preferred_element_type=jnp.float32
    ).astype(jnp.bfloat16)
    partial_sums = jnp.einsum(
        "abr,ae->ebr",
        local.astype(jnp.float32),
        sign_table(blocks_here),
        precision=lax.Precision.HIGHEST,
    )
    my_index = lax.axis_index("tensor")
    for bit_pos in range(lax.axis_size("tensor").bit_length() - 1):
        partner = swapped(partial_sums, "tensor", bit_pos)
        upper = my_index // 2**bit_pos % 2
        partial_sums = jnp.where(upper == 0, partial_sums + partner, partner - partial_sums)
    rotated = (partial_sums * factor).astype(jnp.bfloat16)
    rotated = rotated.reshape(units_here, total_rows)
    weight = dequantize(codes, scales)
    summed = lax.psum_scatter(
        lax.dot_general(
            rotated, weight, (((0,), (0,)), ((), ())), preferred_element_type=jnp.float32
        ),
        "tensor",
        scatter_dimension=0,
        tiled=True,
    )
    return summed.astype(jnp.bfloat16)


def exchanged(value, group_mask, tensor_mask):
    tensor_size = lax.axis_size("tensor")
    pairs = [
        (g * tensor_size + t, (g ^ group_mask) * tensor_size + (t ^ tensor_mask))
        for g in range(lax.axis_size("groups"))
        for t in range(tensor_size)
    ]
    return lax.ppermute(value, AXES, pairs)


def in_hbm(array):
    return pltpu.with_memory_space_constraint(array, pltpu.HBM)


def parity_sign(bits, masks):
    total = jnp.int32(0)
    position = 1
    while position <= masks:
        if masks & position:
            total = total + bits // position % 2
        position *= 2
    return (1 - 2 * (total % 2)).astype(jnp.float32)


def fetches(codes_hbm, group, first, count, words, sems, sem):
    height, tile = words.shape[1:]
    line = pl.multiple_of(group * height, height)
    return [
        pltpu.make_async_copy(
            codes_hbm.at[pl.ds(line, height), pl.ds((first + i) * tile, tile)],
            words.at[i],
            sems.at[sem + i],
        )
        for i in range(count)
    ]


def local_kernel(
    group_ref,
    gate_hbm,
    up_hbm,
    table_hbm,
    scales_hbm,
    out_ref,
    scales_ref,
    gate_in,
    up_in,
    table,
    hidden_sc,
    stack_sc,
    mix_sc,
    sems,
):
    group = group_ref[0]
    copies = [
        pltpu.make_async_copy(source, target, sems.at[index])
        for index, (source, target) in enumerate(
            ((gate_hbm, gate_in), (up_hbm, up_in), (table_hbm, table), (scales_hbm, scales_ref))
        )
    ]
    for copy in copies:
        copy.start()
    rows = gate_in.shape[0]
    blocks = gate_in.shape[1] // HAD_LOCAL
    half = blocks // 2
    line = lax.broadcasted_iota(jnp.int32, (blocks * rows, blocks * rows), 0)
    column = lax.broadcasted_iota(jnp.int32, (blocks * rows, blocks * rows), 1)
    common = (line // rows) & (column // rows)
    odd = jnp.zeros_like(common)
    for bit_pos in range(blocks.bit_length() - 1):
        odd = odd ^ ((common >> bit_pos) & 1)
    walsh = jnp.where(line % rows == column % rows, 1 - 2 * odd, 0)
    walsh = walsh.astype(jnp.float32).astype(jnp.bfloat16)
    copies[0].wait()
    copies[1].wait()
    gate = gate_in[...].astype(jnp.float32)
    hidden_sc[...] = gate / (1.0 + jnp.exp(-gate)) * up_in[...].astype(jnp.float32)
    for a in range(blocks):
        stack_sc[a * rows : (a + 1) * rows, :] = hidden_sc[
            :, a * HAD_LOCAL : (a + 1) * HAD_LOCAL
        ].astype(jnp.bfloat16)
    copies[2].wait()
    hidden = stack_sc[...]
    wide = table.shape[0] // HAD_LOCAL
    for piece in range(wide):
        local = jnp.dot(
            hidden,
            table[piece * HAD_LOCAL : (piece + 1) * HAD_LOCAL, :],
            preferred_element_type=jnp.float32,
        ).astype(jnp.bfloat16)
        mix_sc[:, piece * LANES : (piece + 1) * LANES] = jnp.dot(
            walsh, local, preferred_element_type=jnp.float32
        ).astype(jnp.bfloat16)
    padded = wide * LANES // 2
    for part in range(2):
        first = (group if part == 0 else 1 - group) * half
        for parity in range(2):
            for e in range(half):
                start = pl.multiple_of((first + e) * rows, rows)
                offset = (parity * half + e) * PAIRS
                out_ref[part, :, offset : offset + PAIRS] = mix_sc[
                    pl.ds(start, rows), parity * padded : parity * padded + PAIRS
                ]
    copies[3].wait()


def local_rotation(group, gate_act, up_act, scales):
    units, rows = gate_act.shape
    blocks = units // HAD_LOCAL
    padded = -(-PAIRS // LANES) * LANES
    by_parity = local_matrix(HAD_LOCAL).reshape(PAIRS, 2, HAD_LOCAL)
    table = np.zeros((HAD_LOCAL, 2 * padded), np.float32)
    table[:, :PAIRS] = by_parity[:, 0].T
    table[:, padded : padded + PAIRS] = by_parity[:, 1].T
    table = np.concatenate(np.split(table, 2 * padded // LANES, axis=1))
    hbm = pl.BlockSpec(memory_space=pltpu.HBM)
    vmem = pl.BlockSpec(memory_space=pltpu.VMEM)
    return pl.pallas_call(
        local_kernel,
        in_specs=[pl.BlockSpec(memory_space=pltpu.SMEM)] + [hbm] * 4,
        out_specs=[vmem, vmem],
        out_shape=[
            jax.ShapeDtypeStruct((2, rows, units // 2), jnp.bfloat16),
            pltpu.VMEM(scales.shape, scales.dtype),
        ],
        scratch_shapes=[
            pltpu.VMEM((rows, units), jnp.bfloat16),
            pltpu.VMEM((rows, units), jnp.bfloat16),
            pltpu.VMEM(table.shape, jnp.bfloat16),
            pltpu.VMEM((rows, units), jnp.float32),
            pltpu.VMEM((blocks * rows, HAD_LOCAL), jnp.bfloat16),
            pltpu.VMEM((blocks * rows, 2 * padded), jnp.bfloat16),
            pltpu.SemaphoreType.DMA((4,)),
        ],
        compiler_params=pltpu.CompilerParams(vmem_limit_bytes=6 * MIB),
        cost_estimate=pl.CostEstimate(flops=10**8, bytes_accessed=8 * MIB, transcendentals=10**5),
        name="local_rotation",
    )(
        group,
        in_hbm(gate_act.T),
        in_hbm(up_act.T),
        in_hbm(jnp.asarray(table, jnp.bfloat16)),
        in_hbm(scales),
    )


def unpack_span(words, scale):
    scale = jnp.broadcast_to(scale, words.shape).astype(jnp.bfloat16)
    eight = jnp.bfloat16(8)
    low = (words & 15).astype(jnp.float32).astype(jnp.bfloat16)
    high = (words >> 4).astype(jnp.float32).astype(jnp.bfloat16)
    return (low - eight) * scale, (high - eight) * scale


def widen(group, scales_ref, wide_ref):
    per = wide_ref.shape[0]
    for part in range(2):

        @pl.when(group == part)
        def _(part=part):
            wide_ref[...] = scales_ref[part * per : (part + 1) * per, :].astype(jnp.float32)


def unpack_tile(words, scales_ref, column, target, at, spans):
    height, tile = words.shape
    for p in spans:
        top = p * WORDS_PER_GROUP
        low, high = unpack_span(
            words[top : top + WORDS_PER_GROUP, :], scales_ref[p : p + 1, pl.ds(column, tile)]
        )
        target[top : top + WORDS_PER_GROUP, pl.ds(at, tile)] = low
        target[height + top : height + top + WORDS_PER_GROUP, pl.ds(at, tile)] = high


def first_kernel(group_ref, codes_hbm, scales_in, out_ref, next_ref, wide_ref, words, sems):
    group = group_ref[0]
    own, height, tile = words.shape
    ahead = next_ref.shape[0]
    copies = fetches(codes_hbm, group, 0, own, words, sems, 0)
    copies += fetches(codes_hbm, group, own, ahead, next_ref, sems, own)
    for copy in copies:
        copy.start()
    widen(group, scales_in, wide_ref)
    for i in range(own):
        copies[i].wait()
        unpack_tile(
            words.at[i], wide_ref, i * tile, out_ref, i * tile, range(height // WORDS_PER_GROUP)
        )
    for copy in copies[own:]:
        copy.wait()


def first_unpack(group, codes, scales, own, ahead):
    words, width = codes.shape
    hbm = pl.BlockSpec(memory_space=pltpu.HBM)
    vmem = pl.BlockSpec(memory_space=pltpu.VMEM)
    return pl.pallas_call(
        first_kernel,
        in_specs=[pl.BlockSpec(memory_space=pltpu.SMEM), hbm, vmem],
        out_specs=[vmem] * 3,
        out_shape=[
            pltpu.VMEM((words, own * TILE), jnp.bfloat16),
            pltpu.VMEM((ahead, words // 2, TILE), codes.dtype),
            pltpu.VMEM((words // 2 // WORDS_PER_GROUP, width), jnp.float32),
        ],
        scratch_shapes=[
            pltpu.VMEM((own, words // 2, TILE), codes.dtype),
            pltpu.SemaphoreType.DMA((own + ahead,)),
        ],
        compiler_params=pltpu.CompilerParams(vmem_limit_bytes=(2 + 2 * own) * MIB),
        cost_estimate=pl.CostEstimate(
            flops=0, bytes_accessed=(own + ahead) * words * TILE * 2, transcendentals=0
        ),
        name="first_unpack",
    )(group, in_hbm(codes), pltpu.with_memory_space_constraint(scales, pltpu.VMEM))


def unpack_kernel(first, group_ref, codes_hbm, scales_ref, given, out_ref, next_ref, words, sems):
    group = group_ref[0]
    count, height, tile = given.shape
    own, ahead = words.shape[0], next_ref.shape[0]
    copies = fetches(codes_hbm, group, first + count, own, words, sems, 0)
    copies += fetches(codes_hbm, group, first + count + own, ahead, next_ref, sems, own)
    for copy in copies:
        copy.start()
    spans = range(height // WORDS_PER_GROUP)

    @pl.loop(0, count)
    def _(i):
        at = pl.multiple_of(i * tile, tile)
        unpack_tile(given.at[i], scales_ref, first * tile + at, out_ref, at, spans)

    @pl.loop(0, own)
    def _(i):
        pltpu.make_async_copy(
            codes_hbm.at[pl.ds(0, height), pl.ds(0, tile)], words.at[i], sems.at[i]
        ).wait()
        at = pl.multiple_of((count + i) * tile, tile)
        unpack_tile(words.at[i], scales_ref, first * tile + at, out_ref, at, spans)

    for copy in copies[own:]:
        copy.wait()


def unpack(group, codes, scales, given, first, own, ahead):
    words = codes.shape[0]
    hbm = pl.BlockSpec(memory_space=pltpu.HBM)
    vmem = pl.BlockSpec(memory_space=pltpu.VMEM)
    columns = (given.shape[0] + own) * TILE
    return pl.pallas_call(
        functools.partial(unpack_kernel, first),
        in_specs=[pl.BlockSpec(memory_space=pltpu.SMEM), hbm, vmem, vmem],
        out_specs=[vmem, vmem],
        out_shape=[
            pltpu.VMEM((words, columns), jnp.bfloat16),
            pltpu.VMEM((ahead, words // 2, TILE), codes.dtype),
        ],
        scratch_shapes=[
            pltpu.VMEM((own, words // 2, TILE), codes.dtype),
            pltpu.SemaphoreType.DMA((own + ahead,)),
        ],
        compiler_params=pltpu.CompilerParams(vmem_limit_bytes=(2 + 2 * own) * MIB),
        cost_estimate=pl.CostEstimate(
            flops=words * columns * 8, bytes_accessed=words * columns * 4, transcendentals=0
        ),
        name="unpack",
    )(
        group,
        in_hbm(codes),
        pltpu.with_memory_space_constraint(scales, pltpu.VMEM),
        pltpu.with_memory_space_constraint(given, pltpu.VMEM),
    )


def product_kernel(readies, place_ref, codes_hbm, given, scales_ref, own_ref, *refs):
    *others, keep_ref, send_ref, first_sc, second_sc, words, sems = refs
    ready_refs, others = others[:readies], others[readies:]
    rows = own_ref.shape[0]
    group, place = place_ref[0], place_ref[1]
    held, height, tile = given.shape
    ready_tiles = [
        (ref, i * tile) for ref in ready_refs for i in range(ref.shape[1] // tile)
    ]
    tiles = scales_ref.shape[1] // tile
    base = len(ready_tiles)
    own = tiles - base - held
    copies = fetches(codes_hbm, group, base + held, own, words, sems, 0)
    for copy in copies:
        copy.start()

    count = len(others) + 1
    far = 4 * (count - 1)
    total = own_ref[...].astype(jnp.float32) * parity_sign(place, far)
    for index, other in enumerate(others):
        total = total + other[...].astype(jnp.float32) * parity_sign(
            place & (place ^ (4 * (count - 1 - index))), far
        )
    rotated = (total * (1.0 / math.sqrt(HAD_CROSS))).astype(jnp.bfloat16)
    each = rows // (8 * count)
    slot = lax.broadcasted_iota(jnp.int32, (rows, rows), 0)
    column = lax.broadcasted_iota(jnp.int32, (rows, rows), 1)
    unit = slot // each
    away = unit // (4 * count) + 2 * (unit // count % 2) + 4 * (unit % count)
    source = (unit // (2 * count) % 2) * (rows // 2) + (away ^ place) * each + slot % each
    pick = (column == source).astype(jnp.float32).astype(jnp.bfloat16)
    rotated = jnp.dot(pick, rotated, preferred_element_type=jnp.float32).astype(jnp.bfloat16)

    depth = rotated.shape[1]
    spans = height // WORDS_PER_GROUP
    cuts = list(range(0, depth, CHUNK)) + [depth]

    def stage(products, fresh):
        sums = [None] * len(products)
        done = 0
        for k, (low, high) in enumerate(zip(cuts[:-1], cuts[1:])):
            for index, (weight, at, _) in enumerate(products):
                part = jnp.dot(
                    rotated[:, low:high],
                    weight[low:high, at : at + tile],
                    preferred_element_type=jnp.float32,
                )
                sums[index] = sums[index] + part if k else part
            if fresh is not None:
                source, column, target = fresh
                upto = spans * (k + 1) // (len(cuts) - 1)
                unpack_tile(source, scales_ref, column, target, 0, range(done, upto))
                done = upto
        for total, (_, _, to) in zip(sums, products):
            keep_ref[:, to : to + tile] = total[: rows // 2]
            send_ref[:, to : to + tile] = total[rows // 2 :].astype(jnp.bfloat16)

    waiting = [(ref, at, index * tile) for index, (ref, at) in enumerate(ready_tiles)]
    each_stage = -(-base // (tiles - base))
    previous = None
    for index in range(base, tiles):
        number = index - base
        if number >= held:
            copies[number - held].wait()
        source = given.at[number] if number < held else words.at[number - held]
        target = second_sc if number % 2 else first_sc
        products = waiting[:each_stage]
        waiting = waiting[each_stage:]
        if previous is not None:
            products.append(previous)
        stage(products, (source, index * tile, target))
        previous = (target, 0, index * tile)
    stage(waiting + [previous], None)


def product(place, codes, given, scales, own, others, ready):
    rows = own.shape[0]
    words, width = codes.shape
    hbm = pl.BlockSpec(memory_space=pltpu.HBM)
    vmem = pl.BlockSpec(memory_space=pltpu.VMEM)
    left = width // TILE - given.shape[0] - sum(r.shape[1] for r in ready) // TILE
    held = [pltpu.with_memory_space_constraint(r, pltpu.VMEM) for r in (given, scales)]
    return pl.pallas_call(
        functools.partial(product_kernel, len(ready)),
        in_specs=[pl.BlockSpec(memory_space=pltpu.SMEM), hbm]
        + [vmem] * (3 + len(ready) + len(others)),
        out_specs=[vmem, vmem],
        out_shape=[
            jax.ShapeDtypeStruct((rows // 2, width), jnp.float32),
            jax.ShapeDtypeStruct((rows // 2, width), jnp.bfloat16),
        ],
        scratch_shapes=[
            pltpu.VMEM((words, TILE), jnp.bfloat16),
            pltpu.VMEM((words, TILE), jnp.bfloat16),
            pltpu.VMEM((max(left, 1), words // 2, TILE), codes.dtype),
            pltpu.SemaphoreType.DMA((max(left, 1),)),
        ],
        compiler_params=pltpu.CompilerParams(vmem_limit_bytes=(8 + 2 * left) * MIB),
        name="product",
    )(
        place,
        in_hbm(codes),
        *held,
        own,
        *[pltpu.with_memory_space_constraint(r, pltpu.VMEM) for r in ready],
        *others,
    )


def shared_body(gate_act, up_act, codes, scales):
    rows = gate_act.shape[1]
    width = codes.shape[1]
    tensor_size = lax.axis_size("tensor")
    count = tensor_size // 4
    each = rows // tensor_size
    group = lax.axis_index("groups").astype(jnp.int32)[None]
    place = lax.axis_index("tensor").astype(jnp.int32)[None]

    tiles = width // TILE
    at_near, for_far, at_far, for_product = (tiles * n // 16 for n in FETCHES)
    parts, scales = local_rotation(group, gate_act, up_act, scales)
    near = exchanged(parts, 0, 1)
    core = place[0] % 2
    parts = jnp.where(
        core == 0,
        parts.astype(jnp.float32) + near.astype(jnp.float32),
        near.astype(jnp.float32) - parts.astype(jnp.float32),
    ).astype(jnp.bfloat16)
    parts, group_then = lax.optimization_barrier((parts, group))
    mine, theirs = parts[0], parts[1]
    across_y = exchanged(mine, 0, 2).astype(jnp.float32)
    across_xy = exchanged(theirs, 1, 2).astype(jnp.float32)
    across_x = exchanged(theirs, 1, 0).astype(jnp.float32)
    early, words, scales = first_unpack(group_then, codes, scales, at_near, for_far)
    sign = jnp.where(place[0] // 2 % 2 == 0, 1.0, -1.0)
    both = jnp.concatenate(
        [mine.astype(jnp.float32) * sign + across_y, across_xy + across_x * sign]
    ).astype(jnp.bfloat16)
    both, group_then, words = lax.optimization_barrier((both, group, words))
    others = [exchanged(both, 0, 4 * d) for d in range(count - 1, 0, -1)]
    late, words = unpack(group_then, codes, scales, words, at_near, at_far, for_product)
    keep, send = product(
        jnp.concatenate([group, place]), codes, words, scales, both, others, [early, late]
    )

    keep = keep + exchanged(send, 0, 1).astype(jnp.float32)
    quarters = keep.reshape(4, count * each, width)
    send = quarters[1:].astype(jnp.bfloat16)
    keep = (
        quarters[0]
        + exchanged(send[0], 0, 2).astype(jnp.float32)
        + exchanged(send[1], 1, 0).astype(jnp.float32)
        + exchanged(send[2], 1, 2).astype(jnp.float32)
    )
    send = keep.astype(jnp.bfloat16)
    total = keep[:each]
    for d in range(count - 1, 0, -1):
        total = total + exchanged(send[d * each : (d + 1) * each], 0, 4 * d).astype(jnp.float32)
    return total.astype(jnp.bfloat16)


def body(gate_act, up_act, codes, scales):
    tensor_size = lax.axis_size("tensor")
    blocks = gate_act.shape[0] // HAD_LOCAL
    if (
        lax.axis_size("groups") == 2
        and tensor_size >= 4
        and blocks % 2 == 0
        and gate_act.shape[1] % tensor_size == 0
        and blocks * gate_act.shape[1] <= 128
        and codes.shape[1] % (16 * TILE) == 0
    ):
        return shared_body(gate_act, up_act, codes, scales)
    return general_body(gate_act, up_act, codes, scales)


def solution(mesh):
    placed = (P("tensor", "groups"), P("tensor", "groups"), P("tensor", None), P("tensor", None))
    return jax.shard_map(
        body, mesh=mesh, in_specs=placed, out_specs=P(("groups", "tensor"), None), check_vma=False
    )
```

```python
import functools
import math

import jax
import jax.numpy as jnp
import numpy as np
from jax import lax
from jax.experimental import pallas as pl
from jax.experimental.pallas import tpu as pltpu
from jax.sharding import PartitionSpec as P

HAD_CROSS = 128
GROUP = 32
HAD_LOCAL = 416
PAIRS = HAD_LOCAL // 2
WORDS_PER_GROUP = GROUP // 2
AXES = ("groups", "tensor")
MIB = 2**20
TILE = 512
CHUNK = 128
FETCHES = (1, 2, 7, 3)
LANES = 128


def paley_table():
    squares = set()
    for real_part in range(5):
        for root_part in range(5):
            squares.add(
                (
                    (real_part * real_part + 2 * root_part * root_part) % 5,
                    2 * real_part * root_part % 5,
                )
            )
    jacobsthal = np.zeros((25, 25))
    for first in range(25):
        for second in range(25):
            differ = ((first // 5 - second // 5) % 5, (first % 5 - second % 5) % 5)
            if differ == (0, 0):
                jacobsthal[first, second] = 0.0
            elif differ in squares:
                jacobsthal[first, second] = 1.0
            else:
                jacobsthal[first, second] = -1.0
    conference = np.zeros((26, 26))
    conference[0, 1:] = 1.0
    conference[1:, 0] = 1.0
    conference[1:, 1:] = jacobsthal
    return np.kron(conference, np.array([[1.0, 1.0], [1.0, -1.0]])) + np.kron(
        np.eye(26), np.array([[1.0, -1.0], [-1.0, -1.0]])
    )


def walsh_table(order):
    matrix = np.ones((1, 1))
    while matrix.shape[0] < order:
        matrix = np.kron(np.array([[1.0, 1.0], [1.0, -1.0]]), matrix)
    return matrix


def local_matrix(order):
    return np.kron(walsh_table(order // 52), paley_table()) / math.sqrt(order)


def hadamard_local(order):
    return jnp.asarray(local_matrix(order), dtype=jnp.float32).astype(jnp.bfloat16)


def sign_table(order):
    return jnp.asarray(walsh_table(order), dtype=jnp.float32)


def swapped(value, axis, distance):
    mask = 2**distance
    pairs = [(source, source ^ mask) for source in range(lax.axis_size(axis))]
    return lax.ppermute(value, axis, pairs)


def dequantize(words, group_scales):
    low_codes = words % 16
    high_codes = words // 16
    unpacked = jnp.stack([low_codes, high_codes], axis=1).reshape(
        2 * words.shape[0], words.shape[1]
    )
    spread = jnp.repeat(group_scales.astype(jnp.float32), GROUP, axis=0)
    return ((unpacked - 8).astype(jnp.float32) * spread).astype(jnp.bfloat16)


def general_body(gate_act, up_act, codes, scales):
    units_here = gate_act.shape[0]
    total_rows = gate_act.shape[1]
    blocks_here = units_here // HAD_LOCAL
    factor = 1.0 / math.sqrt(HAD_CROSS)
    hidden = (jax.nn.silu(gate_act.astype(jnp.float32)) * up_act.astype(jnp.float32)).astype(
        jnp.bfloat16
    )
    hidden = hidden.reshape(blocks_here, HAD_LOCAL, total_rows)
    local = jnp.einsum(
        "kn,anr->akr", hadamard_local(HAD_LOCAL), hidden, preferred_element_type=jnp.float32
    ).astype(jnp.bfloat16)
    partial_sums = jnp.einsum(
        "abr,ae->ebr",
        local.astype(jnp.float32),
        sign_table(blocks_here),
        precision=lax.Precision.HIGHEST,
    )
    my_index = lax.axis_index("tensor")
    for bit_pos in range(lax.axis_size("tensor").bit_length() - 1):
        partner = swapped(partial_sums, "tensor", bit_pos)
        upper = my_index // 2**bit_pos % 2
        partial_sums = jnp.where(upper == 0, partial_sums + partner, partner - partial_sums)
    rotated = (partial_sums * factor).astype(jnp.bfloat16)
    rotated = rotated.reshape(units_here, total_rows)
    weight = dequantize(codes, scales)
    summed = lax.psum_scatter(
        lax.dot_general(
            rotated, weight, (((0,), (0,)), ((), ())), preferred_element_type=jnp.float32
        ),
        "tensor",
        scatter_dimension=0,
        tiled=True,
    )
    return summed.astype(jnp.bfloat16)


def exchanged(value, group_mask, tensor_mask):
    tensor_size = lax.axis_size("tensor")
    pairs = [
        (g * tensor_size + t, (g ^ group_mask) * tensor_size + (t ^ tensor_mask))
        for g in range(lax.axis_size("groups"))
        for t in range(tensor_size)
    ]
    return lax.ppermute(value, AXES, pairs)


def start_order(count):
    return [count // 2] + [d for d in range(count - 1, 0, -1) if d != count // 2]


def in_hbm(array):
    return pltpu.with_memory_space_constraint(array, pltpu.HBM)


def parity_sign(bits, masks):
    total = jnp.int32(0)
    position = 1
    while position <= masks:
        if masks & position:
            total = total + bits // position % 2
        position *= 2
    return (1 - 2 * (total % 2)).astype(jnp.float32)


def fetches(codes_hbm, group, first, count, words, sems, sem):
    height, tile = words.shape[1:]
    line = pl.multiple_of(group * height, height)
    return [
        pltpu.make_async_copy(
            codes_hbm.at[pl.ds(line, height), pl.ds((first + i) * tile, tile)],
            words.at[i],
            sems.at[sem + i],
        )
        for i in range(count)
    ]


def local_kernel(
    group_ref,
    gate_hbm,
    up_hbm,
    table_hbm,
    scales_hbm,
    out_ref,
    scales_ref,
    gate_in,
    up_in,
    table,
    hidden_sc,
    stack_sc,
    mix_sc,
    sems,
):
    group = group_ref[0]
    copies = [
        pltpu.make_async_copy(source, target, sems.at[index])
        for index, (source, target) in enumerate(
            ((gate_hbm, gate_in), (up_hbm, up_in), (table_hbm, table), (scales_hbm, scales_ref))
        )
    ]
    for copy in copies:
        copy.start()
    rows = gate_in.shape[0]
    blocks = gate_in.shape[1] // HAD_LOCAL
    half = blocks // 2
    line = lax.broadcasted_iota(jnp.int32, (blocks * rows, blocks * rows), 0)
    column = lax.broadcasted_iota(jnp.int32, (blocks * rows, blocks * rows), 1)
    common = (line // rows) & (column // rows)
    odd = jnp.zeros_like(common)
    for bit_pos in range(blocks.bit_length() - 1):
        odd = odd ^ ((common >> bit_pos) & 1)
    walsh = jnp.where(line % rows == column % rows, 1 - 2 * odd, 0)
    walsh = walsh.astype(jnp.float32).astype(jnp.bfloat16)
    copies[0].wait()
    copies[1].wait()
    gate = gate_in[...].astype(jnp.float32)
    hidden_sc[...] = gate / (1.0 + jnp.exp(-gate)) * up_in[...].astype(jnp.float32)
    for a in range(blocks):
        stack_sc[a * rows : (a + 1) * rows, :] = hidden_sc[
            :, a * HAD_LOCAL : (a + 1) * HAD_LOCAL
        ].astype(jnp.bfloat16)
    copies[2].wait()
    hidden = stack_sc[...]
    wide = table.shape[0] // HAD_LOCAL
    for piece in range(wide):
        local = jnp.dot(
            hidden,
            table[piece * HAD_LOCAL : (piece + 1) * HAD_LOCAL, :],
            preferred_element_type=jnp.float32,
        ).astype(jnp.bfloat16)
        mix_sc[:, piece * LANES : (piece + 1) * LANES] = jnp.dot(
            walsh, local, preferred_element_type=jnp.float32
        ).astype(jnp.bfloat16)
    padded = wide * LANES // 2
    for part in range(2):
        first = (group if part == 0 else 1 - group) * half
        for parity in range(2):
            for e in range(half):
                start = pl.multiple_of((first + e) * rows, rows)
                offset = (parity * half + e) * PAIRS
                out_ref[part, :, offset : offset + PAIRS] = mix_sc[
                    pl.ds(start, rows), parity * padded : parity * padded + PAIRS
                ]
    copies[3].wait()


def local_rotation(group, gate_act, up_act, scales):
    units, rows = gate_act.shape
    blocks = units // HAD_LOCAL
    padded = -(-PAIRS // LANES) * LANES
    by_parity = local_matrix(HAD_LOCAL).reshape(PAIRS, 2, HAD_LOCAL)
    table = np.zeros((HAD_LOCAL, 2 * padded), np.float32)
    table[:, :PAIRS] = by_parity[:, 0].T
    table[:, padded : padded + PAIRS] = by_parity[:, 1].T
    table = np.concatenate(np.split(table, 2 * padded // LANES, axis=1))
    hbm = pl.BlockSpec(memory_space=pltpu.HBM)
    vmem = pl.BlockSpec(memory_space=pltpu.VMEM)
    return pl.pallas_call(
        local_kernel,
        in_specs=[pl.BlockSpec(memory_space=pltpu.SMEM)] + [hbm] * 4,
        out_specs=[vmem, vmem],
        out_shape=[
            jax.ShapeDtypeStruct((2, rows, units // 2), jnp.bfloat16),
            pltpu.VMEM(scales.shape, scales.dtype),
        ],
        scratch_shapes=[
            pltpu.VMEM((rows, units), jnp.bfloat16),
            pltpu.VMEM((rows, units), jnp.bfloat16),
            pltpu.VMEM(table.shape, jnp.bfloat16),
            pltpu.VMEM((rows, units), jnp.float32),
            pltpu.VMEM((blocks * rows, HAD_LOCAL), jnp.bfloat16),
            pltpu.VMEM((blocks * rows, 2 * padded), jnp.bfloat16),
            pltpu.SemaphoreType.DMA((4,)),
        ],
        compiler_params=pltpu.CompilerParams(vmem_limit_bytes=6 * MIB),
        cost_estimate=pl.CostEstimate(flops=10**8, bytes_accessed=8 * MIB, transcendentals=10**5),
        name="local_rotation",
    )(
        group,
        in_hbm(gate_act.T),
        in_hbm(up_act.T),
        in_hbm(jnp.asarray(table, jnp.bfloat16)),
        in_hbm(scales),
    )


def unpack_span(words, scale):
    scale = jnp.broadcast_to(scale, words.shape).astype(jnp.bfloat16)
    eight = jnp.bfloat16(8)
    low = (words & 15).astype(jnp.float32).astype(jnp.bfloat16)
    high = (words >> 4).astype(jnp.float32).astype(jnp.bfloat16)
    return (low - eight) * scale, (high - eight) * scale


def widen(group, scales_ref, wide_ref):
    per = wide_ref.shape[0]
    for part in range(2):

        @pl.when(group == part)
        def _(part=part):
            wide_ref[...] = scales_ref[part * per : (part + 1) * per, :].astype(jnp.float32)


def unpack_tile(words, scales_ref, column, target, at, spans):
    height, tile = words.shape
    for p in spans:
        top = p * WORDS_PER_GROUP
        low, high = unpack_span(
            words[top : top + WORDS_PER_GROUP, :], scales_ref[p : p + 1, pl.ds(column, tile)]
        )
        target[top : top + WORDS_PER_GROUP, pl.ds(at, tile)] = low
        target[height + top : height + top + WORDS_PER_GROUP, pl.ds(at, tile)] = high


def first_kernel(group_ref, codes_hbm, scales_in, out_ref, next_ref, wide_ref, words, sems):
    group = group_ref[0]
    own, height, tile = words.shape
    ahead = next_ref.shape[0]
    copies = fetches(codes_hbm, group, 0, own, words, sems, 0)
    copies += fetches(codes_hbm, group, own, ahead, next_ref, sems, own)
    for copy in copies:
        copy.start()
    widen(group, scales_in, wide_ref)
    for i in range(own):
        copies[i].wait()
        unpack_tile(
            words.at[i], wide_ref, i * tile, out_ref, i * tile, range(height // WORDS_PER_GROUP)
        )
    for copy in copies[own:]:
        copy.wait()


def first_unpack(group, codes, scales, own, ahead):
    words, width = codes.shape
    hbm = pl.BlockSpec(memory_space=pltpu.HBM)
    vmem = pl.BlockSpec(memory_space=pltpu.VMEM)
    return pl.pallas_call(
        first_kernel,
        in_specs=[pl.BlockSpec(memory_space=pltpu.SMEM), hbm, vmem],
        out_specs=[vmem] * 3,
        out_shape=[
            pltpu.VMEM((words, own * TILE), jnp.bfloat16),
            pltpu.VMEM((ahead, words // 2, TILE), codes.dtype),
            pltpu.VMEM((words // 2 // WORDS_PER_GROUP, width), jnp.float32),
        ],
        scratch_shapes=[
            pltpu.VMEM((own, words // 2, TILE), codes.dtype),
            pltpu.SemaphoreType.DMA((own + ahead,)),
        ],
        compiler_params=pltpu.CompilerParams(vmem_limit_bytes=(2 + 2 * own) * MIB),
        cost_estimate=pl.CostEstimate(
            flops=0, bytes_accessed=(own + ahead) * words * TILE * 2, transcendentals=0
        ),
        name="first_unpack",
    )(group, in_hbm(codes), pltpu.with_memory_space_constraint(scales, pltpu.VMEM))


def unpack_kernel(first, group_ref, codes_hbm, scales_ref, given, out_ref, next_ref, words, sems):
    group = group_ref[0]
    count, height, tile = given.shape
    own, ahead = words.shape[0], next_ref.shape[0]
    copies = fetches(codes_hbm, group, first + count, own, words, sems, 0)
    copies += fetches(codes_hbm, group, first + count + own, ahead, next_ref, sems, own)
    for copy in copies:
        copy.start()
    spans = range(height // WORDS_PER_GROUP)

    @pl.loop(0, count)
    def _(i):
        at = pl.multiple_of(i * tile, tile)
        unpack_tile(given.at[i], scales_ref, first * tile + at, out_ref, at, spans)

    @pl.loop(0, own)
    def _(i):
        pltpu.make_async_copy(
            codes_hbm.at[pl.ds(0, height), pl.ds(0, tile)], words.at[i], sems.at[i]
        ).wait()
        at = pl.multiple_of((count + i) * tile, tile)
        unpack_tile(words.at[i], scales_ref, first * tile + at, out_ref, at, spans)

    for copy in copies[own:]:
        copy.wait()


def unpack(group, codes, scales, given, first, own, ahead):
    words = codes.shape[0]
    hbm = pl.BlockSpec(memory_space=pltpu.HBM)
    vmem = pl.BlockSpec(memory_space=pltpu.VMEM)
    columns = (given.shape[0] + own) * TILE
    return pl.pallas_call(
        functools.partial(unpack_kernel, first),
        in_specs=[pl.BlockSpec(memory_space=pltpu.SMEM), hbm, vmem, vmem],
        out_specs=[vmem, vmem],
        out_shape=[
            pltpu.VMEM((words, columns), jnp.bfloat16),
            pltpu.VMEM((ahead, words // 2, TILE), codes.dtype),
        ],
        scratch_shapes=[
            pltpu.VMEM((own, words // 2, TILE), codes.dtype),
            pltpu.SemaphoreType.DMA((own + ahead,)),
        ],
        compiler_params=pltpu.CompilerParams(vmem_limit_bytes=(2 + 2 * own) * MIB),
        cost_estimate=pl.CostEstimate(
            flops=words * columns * 8, bytes_accessed=words * columns * 4, transcendentals=0
        ),
        name="unpack",
    )(
        group,
        in_hbm(codes),
        pltpu.with_memory_space_constraint(scales, pltpu.VMEM),
        pltpu.with_memory_space_constraint(given, pltpu.VMEM),
    )


def product_kernel(readies, place_ref, codes_hbm, given, scales_ref, own_ref, *refs):
    *others, keep_ref, send_ref, first_sc, second_sc, words, sems = refs
    ready_refs, others = others[:readies], others[readies:]
    rows = own_ref.shape[0]
    group, place = place_ref[0], place_ref[1]
    held, height, tile = given.shape
    ready_tiles = [
        (ref, i * tile) for ref in ready_refs for i in range(ref.shape[1] // tile)
    ]
    tiles = scales_ref.shape[1] // tile
    base = len(ready_tiles)
    own = tiles - base - held
    copies = fetches(codes_hbm, group, base + held, own, words, sems, 0)
    for copy in copies:
        copy.start()

    count = len(others) + 1
    far = 4 * (count - 1)
    total = own_ref[...].astype(jnp.float32) * parity_sign(place, far)
    for distance, other in zip(range(count - 1, 0, -1), others):
        total = total + other[...].astype(jnp.float32) * parity_sign(
            place & (place ^ (4 * distance)), far
        )
    rotated = (total * (1.0 / math.sqrt(HAD_CROSS))).astype(jnp.bfloat16)
    each = rows // (8 * count)
    slot = lax.broadcasted_iota(jnp.int32, (rows, rows), 0)
    column = lax.broadcasted_iota(jnp.int32, (rows, rows), 1)
    unit = slot // each
    away = unit // (4 * count) + 2 * (unit // count % 2) + 4 * (unit % count)
    source = (unit // (2 * count) % 2) * (rows // 2) + (away ^ place) * each + slot % each
    pick = (column == source).astype(jnp.float32).astype(jnp.bfloat16)
    rotated = jnp.dot(pick, rotated, preferred_element_type=jnp.float32).astype(jnp.bfloat16)

    depth = rotated.shape[1]
    spans = height // WORDS_PER_GROUP
    cuts = list(range(0, depth, CHUNK)) + [depth]

    def stage(products, fresh):
        sums = [None] * len(products)
        done = 0
        for k, (low, high) in enumerate(zip(cuts[:-1], cuts[1:])):
            for index, (weight, at, _) in enumerate(products):
                part = jnp.dot(
                    rotated[:, low:high],
                    weight[low:high, at : at + tile],
                    preferred_element_type=jnp.float32,
                )
                sums[index] = sums[index] + part if k else part
            if fresh is not None:
                source, column, target = fresh
                upto = spans * (k + 1) // (len(cuts) - 1)
                unpack_tile(source, scales_ref, column, target, 0, range(done, upto))
                done = upto
        for total, (_, _, to) in zip(sums, products):
            keep_ref[:, to : to + tile] = total[: rows // 2]
            send_ref[:, to : to + tile] = total[rows // 2 :].astype(jnp.bfloat16)

    waiting = [(ref, at, index * tile) for index, (ref, at) in enumerate(ready_tiles)]
    each_stage = -(-base // (tiles - base))
    previous = None
    for index in range(base, tiles):
        number = index - base
        if number >= held:
            copies[number - held].wait()
        source = given.at[number] if number < held else words.at[number - held]
        target = second_sc if number % 2 else first_sc
        products = waiting[:each_stage]
        waiting = waiting[each_stage:]
        if previous is not None:
            products.append(previous)
        stage(products, (source, index * tile, target))
        previous = (target, 0, index * tile)
    stage(waiting + [previous], None)


def product(place, codes, given, scales, own, others, ready):
    rows = own.shape[0]
    words, width = codes.shape
    hbm = pl.BlockSpec(memory_space=pltpu.HBM)
    vmem = pl.BlockSpec(memory_space=pltpu.VMEM)
    left = width // TILE - given.shape[0] - sum(r.shape[1] for r in ready) // TILE
    held = [pltpu.with_memory_space_constraint(r, pltpu.VMEM) for r in (given, scales)]
    return pl.pallas_call(
        functools.partial(product_kernel, len(ready)),
        in_specs=[pl.BlockSpec(memory_space=pltpu.SMEM), hbm]
        + [vmem] * (3 + len(ready) + len(others)),
        out_specs=[vmem, vmem],
        out_shape=[
            jax.ShapeDtypeStruct((rows // 2, width), jnp.float32),
            jax.ShapeDtypeStruct((rows // 2, width), jnp.bfloat16),
        ],
        scratch_shapes=[
            pltpu.VMEM((words, TILE), jnp.bfloat16),
            pltpu.VMEM((words, TILE), jnp.bfloat16),
            pltpu.VMEM((max(left, 1), words // 2, TILE), codes.dtype),
            pltpu.SemaphoreType.DMA((max(left, 1),)),
        ],
        compiler_params=pltpu.CompilerParams(vmem_limit_bytes=(8 + 2 * left) * MIB),
        name="product",
    )(
        place,
        in_hbm(codes),
        *held,
        own,
        *[pltpu.with_memory_space_constraint(r, pltpu.VMEM) for r in ready],
        *others,
    )


def shared_body(gate_act, up_act, codes, scales):
    rows = gate_act.shape[1]
    width = codes.shape[1]
    tensor_size = lax.axis_size("tensor")
    count = tensor_size // 4
    each = rows // tensor_size
    group = lax.axis_index("groups").astype(jnp.int32)[None]
    place = lax.axis_index("tensor").astype(jnp.int32)[None]

    tiles = width // TILE
    at_near, for_far, at_far, for_product = (tiles * n // 16 for n in FETCHES)
    parts, scales = local_rotation(group, gate_act, up_act, scales)
    near = exchanged(parts, 0, 1)
    core = place[0] % 2
    parts = jnp.where(
        core == 0,
        parts.astype(jnp.float32) + near.astype(jnp.float32),
        near.astype(jnp.float32) - parts.astype(jnp.float32),
    ).astype(jnp.bfloat16)
    parts, group_then = lax.optimization_barrier((parts, group))
    mine, theirs = parts[0], parts[1]
    across_y = exchanged(mine, 0, 2).astype(jnp.float32)
    across_xy = exchanged(theirs, 1, 2).astype(jnp.float32)
    across_x = exchanged(theirs, 1, 0).astype(jnp.float32)
    early, words, scales = first_unpack(group_then, codes, scales, at_near, for_far)
    sign = jnp.where(place[0] // 2 % 2 == 0, 1.0, -1.0)
    both = jnp.concatenate(
        [mine.astype(jnp.float32) * sign + across_y, across_xy + across_x * sign]
    ).astype(jnp.bfloat16)
    both, group_then, words = lax.optimization_barrier((both, group, words))
    others = [exchanged(both, 0, 4 * d) for d in range(count - 1, 0, -1)]
    late, words = unpack(group_then, codes, scales, words, at_near, at_far, for_product)
    keep, send = product(
        jnp.concatenate([group, place]), codes, words, scales, both, others, [early, late]
    )

    keep = keep + exchanged(send, 0, 1).astype(jnp.float32)
    quarters = keep.reshape(4, count * each, width)
    send = quarters[1:].astype(jnp.bfloat16)
    keep = (
        quarters[0]
        + exchanged(send[0], 0, 2).astype(jnp.float32)
        + exchanged(send[1], 1, 0).astype(jnp.float32)
        + exchanged(send[2], 1, 2).astype(jnp.float32)
    )
    send = keep.astype(jnp.bfloat16)
    total = keep[:each]
    for d in start_order(count):
        total = total + exchanged(send[d * each : (d + 1) * each], 0, 4 * d).astype(jnp.float32)
    return total.astype(jnp.bfloat16)


def body(gate_act, up_act, codes, scales):
    tensor_size = lax.axis_size("tensor")
    blocks = gate_act.shape[0] // HAD_LOCAL
    if (
        lax.axis_size("groups") == 2
        and tensor_size >= 4
        and blocks % 2 == 0
        and gate_act.shape[1] % tensor_size == 0
        and blocks * gate_act.shape[1] <= 128
        and codes.shape[1] % (16 * TILE) == 0
    ):
        return shared_body(gate_act, up_act, codes, scales)
    return general_body(gate_act, up_act, codes, scales)


def solution(mesh):
    placed = (P("tensor", "groups"), P("tensor", "groups"), P("tensor", None), P("tensor", None))
    return jax.shard_map(
        body, mesh=mesh, in_specs=placed, out_specs=P(("groups", "tensor"), None), check_vma=False
    )
```

```python
import functools
import math

import jax
import jax.numpy as jnp
import numpy as np
from jax import lax
from jax.experimental import pallas as pl
from jax.experimental.pallas import tpu as pltpu
from jax.sharding import PartitionSpec as P

HAD_CROSS = 128
GROUP = 32
HAD_LOCAL = 416
PAIRS = HAD_LOCAL // 2
WORDS_PER_GROUP = GROUP // 2
AXES = ("groups", "tensor")
MIB = 2**20
TILE = 512
CHUNK = 128
FETCHES = (1, 5, 4, 3)
LANES = 128


def paley_table():
    squares = set()
    for real_part in range(5):
        for root_part in range(5):
            squares.add(
                (
                    (real_part * real_part + 2 * root_part * root_part) % 5,
                    2 * real_part * root_part % 5,
                )
            )
    jacobsthal = np.zeros((25, 25))
    for first in range(25):
        for second in range(25):
            differ = ((first // 5 - second // 5) % 5, (first % 5 - second % 5) % 5)
            if differ == (0, 0):
                jacobsthal[first, second] = 0.0
            elif differ in squares:
                jacobsthal[first, second] = 1.0
            else:
                jacobsthal[first, second] = -1.0
    conference = np.zeros((26, 26))
    conference[0, 1:] = 1.0
    conference[1:, 0] = 1.0
    conference[1:, 1:] = jacobsthal
    return np.kron(conference, np.array([[1.0, 1.0], [1.0, -1.0]])) + np.kron(
        np.eye(26), np.array([[1.0, -1.0], [-1.0, -1.0]])
    )


def walsh_table(order):
    matrix = np.ones((1, 1))
    while matrix.shape[0] < order:
        matrix = np.kron(np.array([[1.0, 1.0], [1.0, -1.0]]), matrix)
    return matrix


def local_matrix(order):
    return np.kron(walsh_table(order // 52), paley_table()) / math.sqrt(order)


def hadamard_local(order):
    return jnp.asarray(local_matrix(order), dtype=jnp.float32).astype(jnp.bfloat16)


def sign_table(order):
    return jnp.asarray(walsh_table(order), dtype=jnp.float32)


def swapped(value, axis, distance):
    mask = 2**distance
    pairs = [(source, source ^ mask) for source in range(lax.axis_size(axis))]
    return lax.ppermute(value, axis, pairs)


def dequantize(words, group_scales):
    low_codes = words % 16
    high_codes = words // 16
    unpacked = jnp.stack([low_codes, high_codes], axis=1).reshape(
        2 * words.shape[0], words.shape[1]
    )
    spread = jnp.repeat(group_scales.astype(jnp.float32), GROUP, axis=0)
    return ((unpacked - 8).astype(jnp.float32) * spread).astype(jnp.bfloat16)


def general_body(gate_act, up_act, codes, scales):
    units_here = gate_act.shape[0]
    total_rows = gate_act.shape[1]
    blocks_here = units_here // HAD_LOCAL
    factor = 1.0 / math.sqrt(HAD_CROSS)
    hidden = (jax.nn.silu(gate_act.astype(jnp.float32)) * up_act.astype(jnp.float32)).astype(
        jnp.bfloat16
    )
    hidden = hidden.reshape(blocks_here, HAD_LOCAL, total_rows)
    local = jnp.einsum(
        "kn,anr->akr", hadamard_local(HAD_LOCAL), hidden, preferred_element_type=jnp.float32
    ).astype(jnp.bfloat16)
    partial_sums = jnp.einsum(
        "abr,ae->ebr",
        local.astype(jnp.float32),
        sign_table(blocks_here),
        precision=lax.Precision.HIGHEST,
    )
    my_index = lax.axis_index("tensor")
    for bit_pos in range(lax.axis_size("tensor").bit_length() - 1):
        partner = swapped(partial_sums, "tensor", bit_pos)
        upper = my_index // 2**bit_pos % 2
        partial_sums = jnp.where(upper == 0, partial_sums + partner, partner - partial_sums)
    rotated = (partial_sums * factor).astype(jnp.bfloat16)
    rotated = rotated.reshape(units_here, total_rows)
    weight = dequantize(codes, scales)
    summed = lax.psum_scatter(
        lax.dot_general(
            rotated, weight, (((0,), (0,)), ((), ())), preferred_element_type=jnp.float32
        ),
        "tensor",
        scatter_dimension=0,
        tiled=True,
    )
    return summed.astype(jnp.bfloat16)


def exchanged(value, group_mask, tensor_mask):
    tensor_size = lax.axis_size("tensor")
    pairs = [
        (g * tensor_size + t, (g ^ group_mask) * tensor_size + (t ^ tensor_mask))
        for g in range(lax.axis_size("groups"))
        for t in range(tensor_size)
    ]
    return lax.ppermute(value, AXES, pairs)


def start_order(count):
    return [count // 2] + [d for d in range(count - 1, 0, -1) if d != count // 2]


def middle_order(count):
    return [count - 1] + list(range(1, count - 1))


def in_hbm(array):
    return pltpu.with_memory_space_constraint(array, pltpu.HBM)


def parity_sign(bits, masks):
    total = jnp.int32(0)
    position = 1
    while position <= masks:
        if masks & position:
            total = total + bits // position % 2
        position *= 2
    return (1 - 2 * (total % 2)).astype(jnp.float32)


def fetches(codes_hbm, group, first, count, words, sems, sem):
    height, tile = words.shape[1:]
    line = pl.multiple_of(group * height, height)
    return [
        pltpu.make_async_copy(
            codes_hbm.at[pl.ds(line, height), pl.ds((first + i) * tile, tile)],
            words.at[i],
            sems.at[sem + i],
        )
        for i in range(count)
    ]


def local_kernel(
    group_ref,
    gate_hbm,
    up_hbm,
    table_hbm,
    scales_hbm,
    out_ref,
    scales_ref,
    gate_in,
    up_in,
    table,
    hidden_sc,
    stack_sc,
    mix_sc,
    sems,
):
    group = group_ref[0]
    copies = [
        pltpu.make_async_copy(source, target, sems.at[index])
        for index, (source, target) in enumerate(
            ((gate_hbm, gate_in), (up_hbm, up_in), (table_hbm, table), (scales_hbm, scales_ref))
        )
    ]
    for copy in copies:
        copy.start()
    rows = gate_in.shape[0]
    blocks = gate_in.shape[1] // HAD_LOCAL
    half = blocks // 2
    line = lax.broadcasted_iota(jnp.int32, (blocks * rows, blocks * rows), 0)
    column = lax.broadcasted_iota(jnp.int32, (blocks * rows, blocks * rows), 1)
    common = (line // rows) & (column // rows)
    odd = jnp.zeros_like(common)
    for bit_pos in range(blocks.bit_length() - 1):
        odd = odd ^ ((common >> bit_pos) & 1)
    walsh = jnp.where(line % rows == column % rows, 1 - 2 * odd, 0)
    walsh = walsh.astype(jnp.float32).astype(jnp.bfloat16)
    copies[0].wait()
    copies[1].wait()
    gate = gate_in[...].astype(jnp.float32)
    hidden_sc[...] = gate / (1.0 + jnp.exp(-gate)) * up_in[...].astype(jnp.float32)
    for a in range(blocks):
        stack_sc[a * rows : (a + 1) * rows, :] = hidden_sc[
            :, a * HAD_LOCAL : (a + 1) * HAD_LOCAL
        ].astype(jnp.bfloat16)
    copies[2].wait()
    hidden = stack_sc[...]
    wide = table.shape[0] // HAD_LOCAL
    for piece in range(wide):
        local = jnp.dot(
            hidden,
            table[piece * HAD_LOCAL : (piece + 1) * HAD_LOCAL, :],
            preferred_element_type=jnp.float32,
        ).astype(jnp.bfloat16)
        mix_sc[:, piece * LANES : (piece + 1) * LANES] = jnp.dot(
            walsh, local, preferred_element_type=jnp.float32
        ).astype(jnp.bfloat16)
    padded = wide * LANES // 2
    for part in range(2):
        first = (group if part == 0 else 1 - group) * half
        for parity in range(2):
            for e in range(half):
                start = pl.multiple_of((first + e) * rows, rows)
                offset = (parity * half + e) * PAIRS
                out_ref[part, :, offset : offset + PAIRS] = mix_sc[
                    pl.ds(start, rows), parity * padded : parity * padded + PAIRS
                ]
    copies[3].wait()


def local_rotation(group, gate_act, up_act, scales):
    units, rows = gate_act.shape
    blocks = units // HAD_LOCAL
    padded = -(-PAIRS // LANES) * LANES
    by_parity = local_matrix(HAD_LOCAL).reshape(PAIRS, 2, HAD_LOCAL)
    table = np.zeros((HAD_LOCAL, 2 * padded), np.float32)
    table[:, :PAIRS] = by_parity[:, 0].T
    table[:, padded : padded + PAIRS] = by_parity[:, 1].T
    table = np.concatenate(np.split(table, 2 * padded // LANES, axis=1))
    hbm = pl.BlockSpec(memory_space=pltpu.HBM)
    vmem = pl.BlockSpec(memory_space=pltpu.VMEM)
    return pl.pallas_call(
        local_kernel,
        in_specs=[pl.BlockSpec(memory_space=pltpu.SMEM)] + [hbm] * 4,
        out_specs=[vmem, vmem],
        out_shape=[
            jax.ShapeDtypeStruct((2, rows, units // 2), jnp.bfloat16),
            pltpu.VMEM(scales.shape, scales.dtype),
        ],
        scratch_shapes=[
            pltpu.VMEM((rows, units), jnp.bfloat16),
            pltpu.VMEM((rows, units), jnp.bfloat16),
            pltpu.VMEM(table.shape, jnp.bfloat16),
            pltpu.VMEM((rows, units), jnp.float32),
            pltpu.VMEM((blocks * rows, HAD_LOCAL), jnp.bfloat16),
            pltpu.VMEM((blocks * rows, 2 * padded), jnp.bfloat16),
            pltpu.SemaphoreType.DMA((4,)),
        ],
        compiler_params=pltpu.CompilerParams(vmem_limit_bytes=6 * MIB),
        cost_estimate=pl.CostEstimate(flops=10**8, bytes_accessed=8 * MIB, transcendentals=10**5),
        name="local_rotation",
    )(
        group,
        in_hbm(gate_act.T),
        in_hbm(up_act.T),
        in_hbm(jnp.asarray(table, jnp.bfloat16)),
        in_hbm(scales),
    )


def unpack_span(words, scale):
    scale = jnp.broadcast_to(scale, words.shape).astype(jnp.bfloat16)
    eight = jnp.bfloat16(8)
    low = (words & 15).astype(jnp.float32).astype(jnp.bfloat16)
    high = (words >> 4).astype(jnp.float32).astype(jnp.bfloat16)
    return (low - eight) * scale, (high - eight) * scale


def widen(group, scales_ref, wide_ref):
    per = wide_ref.shape[0]
    for part in range(2):

        @pl.when(group == part)
        def _(part=part):
            wide_ref[...] = scales_ref[part * per : (part + 1) * per, :].astype(jnp.float32)


def unpack_tile(words, scales_ref, column, target, at, spans):
    height, tile = words.shape
    for p in spans:
        top = p * WORDS_PER_GROUP
        low, high = unpack_span(
            words[top : top + WORDS_PER_GROUP, :], scales_ref[p : p + 1, pl.ds(column, tile)]
        )
        target[top : top + WORDS_PER_GROUP, pl.ds(at, tile)] = low
        target[height + top : height + top + WORDS_PER_GROUP, pl.ds(at, tile)] = high


def first_kernel(group_ref, codes_hbm, scales_in, out_ref, next_ref, wide_ref, words, sems):
    group = group_ref[0]
    own, height, tile = words.shape
    ahead = next_ref.shape[0]
    copies = fetches(codes_hbm, group, 0, own, words, sems, 0)
    copies += fetches(codes_hbm, group, own, ahead, next_ref, sems, own)
    for copy in copies:
        copy.start()
    widen(group, scales_in, wide_ref)
    for i in range(own):
        copies[i].wait()
        unpack_tile(
            words.at[i], wide_ref, i * tile, out_ref, i * tile, range(height // WORDS_PER_GROUP)
        )
    for copy in copies[own:]:
        copy.wait()


def first_unpack(group, codes, scales, own, ahead):
    words, width = codes.shape
    hbm = pl.BlockSpec(memory_space=pltpu.HBM)
    vmem = pl.BlockSpec(memory_space=pltpu.VMEM)
    return pl.pallas_call(
        first_kernel,
        in_specs=[pl.BlockSpec(memory_space=pltpu.SMEM), hbm, vmem],
        out_specs=[vmem] * 3,
        out_shape=[
            pltpu.VMEM((words, own * TILE), jnp.bfloat16),
            pltpu.VMEM((ahead, words // 2, TILE), codes.dtype),
            pltpu.VMEM((words // 2 // WORDS_PER_GROUP, width), jnp.float32),
        ],
        scratch_shapes=[
            pltpu.VMEM((own, words // 2, TILE), codes.dtype),
            pltpu.SemaphoreType.DMA((own + ahead,)),
        ],
        compiler_params=pltpu.CompilerParams(vmem_limit_bytes=(2 + 2 * own) * MIB),
        cost_estimate=pl.CostEstimate(
            flops=0, bytes_accessed=(own + ahead) * words * TILE * 2, transcendentals=0
        ),
        name="first_unpack",
    )(group, in_hbm(codes), pltpu.with_memory_space_constraint(scales, pltpu.VMEM))


def unpack_kernel(first, group_ref, codes_hbm, scales_ref, given, out_ref, next_ref, words, sems):
    group = group_ref[0]
    count, height, tile = given.shape
    own, ahead = words.shape[0], next_ref.shape[0]
    copies = fetches(codes_hbm, group, first + count, own, words, sems, 0)
    copies += fetches(codes_hbm, group, first + count + own, ahead, next_ref, sems, own)
    for copy in copies:
        copy.start()
    spans = range(height // WORDS_PER_GROUP)

    @pl.loop(0, count)
    def _(i):
        at = pl.multiple_of(i * tile, tile)
        unpack_tile(given.at[i], scales_ref, first * tile + at, out_ref, at, spans)

    @pl.loop(0, own)
    def _(i):
        pltpu.make_async_copy(
            codes_hbm.at[pl.ds(0, height), pl.ds(0, tile)], words.at[i], sems.at[i]
        ).wait()
        at = pl.multiple_of((count + i) * tile, tile)
        unpack_tile(words.at[i], scales_ref, first * tile + at, out_ref, at, spans)

    for copy in copies[own:]:
        copy.wait()


def unpack(group, codes, scales, given, first, own, ahead):
    words = codes.shape[0]
    hbm = pl.BlockSpec(memory_space=pltpu.HBM)
    vmem = pl.BlockSpec(memory_space=pltpu.VMEM)
    columns = (given.shape[0] + own) * TILE
    return pl.pallas_call(
        functools.partial(unpack_kernel, first),
        in_specs=[pl.BlockSpec(memory_space=pltpu.SMEM), hbm, vmem, vmem],
        out_specs=[vmem, vmem],
        out_shape=[
            pltpu.VMEM((words, columns), jnp.bfloat16),
            pltpu.VMEM((ahead, words // 2, TILE), codes.dtype),
        ],
        scratch_shapes=[
            pltpu.VMEM((own, words // 2, TILE), codes.dtype),
            pltpu.SemaphoreType.DMA((own + ahead,)),
        ],
        compiler_params=pltpu.CompilerParams(vmem_limit_bytes=(2 + 2 * own) * MIB),
        cost_estimate=pl.CostEstimate(
            flops=words * columns * 8, bytes_accessed=words * columns * 4, transcendentals=0
        ),
        name="unpack",
    )(
        group,
        in_hbm(codes),
        pltpu.with_memory_space_constraint(scales, pltpu.VMEM),
        pltpu.with_memory_space_constraint(given, pltpu.VMEM),
    )


def product_kernel(readies, place_ref, codes_hbm, given, scales_ref, own_ref, *refs):
    *others, keep_ref, send_ref, first_sc, second_sc, words, sems = refs
    ready_refs, others = others[:readies], others[readies:]
    rows = own_ref.shape[0]
    group, place = place_ref[0], place_ref[1]
    held, height, tile = given.shape
    ready_tiles = [
        (ref, i * tile) for ref in ready_refs for i in range(ref.shape[1] // tile)
    ]
    tiles = scales_ref.shape[1] // tile
    base = len(ready_tiles)
    own = tiles - base - held
    copies = fetches(codes_hbm, group, base + held, own, words, sems, 0)
    for copy in copies:
        copy.start()

    count = len(others) + 1
    middle = 2 * (count - 1)
    total = own_ref[...].astype(jnp.float32) * parity_sign(place, middle)
    for distance, other in zip(middle_order(count), others):
        total = total + other[...].astype(jnp.float32) * parity_sign(
            place & (place ^ (2 * distance)), middle
        )
    rotated = (total * (1.0 / math.sqrt(HAD_CROSS))).astype(jnp.bfloat16)
    each = rows // (8 * count)
    slot = lax.broadcasted_iota(jnp.int32, (rows, rows), 0)
    column = lax.broadcasted_iota(jnp.int32, (rows, rows), 1)
    unit = slot // each
    away = unit // (4 * count) + 2 * (unit // count % 2) + 4 * (unit % count)
    source = (unit // (2 * count) % 2) * (rows // 2) + (away ^ place) * each + slot % each
    pick = (column == source).astype(jnp.float32).astype(jnp.bfloat16)
    rotated = jnp.dot(pick, rotated, preferred_element_type=jnp.float32).astype(jnp.bfloat16)

    depth = rotated.shape[1]
    spans = height // WORDS_PER_GROUP
    cuts = list(range(0, depth, CHUNK)) + [depth]

    def stage(products, fresh):
        sums = [None] * len(products)
        done = 0
        for k, (low, high) in enumerate(zip(cuts[:-1], cuts[1:])):
            for index, (weight, at, _) in enumerate(products):
                part = jnp.dot(
                    rotated[:, low:high],
                    weight[low:high, at : at + tile],
                    preferred_element_type=jnp.float32,
                )
                sums[index] = sums[index] + part if k else part
            if fresh is not None:
                source, column, target = fresh
                upto = spans * (k + 1) // (len(cuts) - 1)
                unpack_tile(source, scales_ref, column, target, 0, range(done, upto))
                done = upto
        for total, (_, _, to) in zip(sums, products):
            keep_ref[:, to : to + tile] = total[: rows // 2]
            send_ref[:, to : to + tile] = total[rows // 2 :].astype(jnp.bfloat16)

    waiting = [(ref, at, index * tile) for index, (ref, at) in enumerate(ready_tiles)]
    each_stage = -(-base // (tiles - base))
    previous = None
    for index in range(base, tiles):
        number = index - base
        if number >= held:
            copies[number - held].wait()
        source = given.at[number] if number < held else words.at[number - held]
        target = second_sc if number % 2 else first_sc
        products = waiting[:each_stage]
        waiting = waiting[each_stage:]
        if previous is not None:
            products.append(previous)
        stage(products, (source, index * tile, target))
        previous = (target, 0, index * tile)
    stage(waiting + [previous], None)


def product(place, codes, given, scales, own, others, ready):
    rows = own.shape[0]
    words, width = codes.shape
    hbm = pl.BlockSpec(memory_space=pltpu.HBM)
    vmem = pl.BlockSpec(memory_space=pltpu.VMEM)
    left = width // TILE - given.shape[0] - sum(r.shape[1] for r in ready) // TILE
    held = [pltpu.with_memory_space_constraint(r, pltpu.VMEM) for r in (given, scales)]
    return pl.pallas_call(
        functools.partial(product_kernel, len(ready)),
        in_specs=[pl.BlockSpec(memory_space=pltpu.SMEM), hbm]
        + [vmem] * (3 + len(ready) + len(others)),
        out_specs=[vmem, vmem],
        out_shape=[
            jax.ShapeDtypeStruct((rows // 2, width), jnp.float32),
            jax.ShapeDtypeStruct((rows // 2, width), jnp.bfloat16),
        ],
        scratch_shapes=[
            pltpu.VMEM((words, TILE), jnp.bfloat16),
            pltpu.VMEM((words, TILE), jnp.bfloat16),
            pltpu.VMEM((max(left, 1), words // 2, TILE), codes.dtype),
            pltpu.SemaphoreType.DMA((max(left, 1),)),
        ],
        compiler_params=pltpu.CompilerParams(vmem_limit_bytes=(8 + 2 * left) * MIB),
        name="product",
    )(
        place,
        in_hbm(codes),
        *held,
        own,
        *[pltpu.with_memory_space_constraint(r, pltpu.VMEM) for r in ready],
        *others,
    )


def shared_body(gate_act, up_act, codes, scales):
    rows = gate_act.shape[1]
    width = codes.shape[1]
    tensor_size = lax.axis_size("tensor")
    count = tensor_size // 4
    each = rows // tensor_size
    group = lax.axis_index("groups").astype(jnp.int32)[None]
    place = lax.axis_index("tensor").astype(jnp.int32)[None]

    tiles = width // TILE
    at_near, for_far, at_far, for_product = (tiles * n // 16 for n in FETCHES)
    parts, scales = local_rotation(group, gate_act, up_act, scales)
    near = exchanged(parts, 0, 1)
    core = place[0] % 2
    parts = jnp.where(
        core == 0,
        parts.astype(jnp.float32) + near.astype(jnp.float32),
        near.astype(jnp.float32) - parts.astype(jnp.float32),
    ).astype(jnp.bfloat16)
    parts, group_then = lax.optimization_barrier((parts, group))
    mine, theirs = parts[0], parts[1]
    top = tensor_size // 2
    across = exchanged(mine, 0, top).astype(jnp.float32)
    across_both = exchanged(theirs, 1, top).astype(jnp.float32)
    across_groups = exchanged(theirs, 1, 0).astype(jnp.float32)
    early, words, scales = first_unpack(group_then, codes, scales, at_near, for_far)
    sign = jnp.where(place[0] // top % 2 == 0, 1.0, -1.0)
    both = jnp.concatenate(
        [mine.astype(jnp.float32) * sign + across, across_both + across_groups * sign]
    ).astype(jnp.bfloat16)
    both, group_then, words = lax.optimization_barrier((both, group, words))
    others = [exchanged(both, 0, 2 * d) for d in middle_order(count)]
    late, words = unpack(group_then, codes, scales, words, at_near, at_far, for_product)
    keep, send = product(
        jnp.concatenate([group, place]), codes, words, scales, both, others, [early, late]
    )

    keep = keep + exchanged(send, 0, 1).astype(jnp.float32)
    quarters = keep.reshape(4, count * each, width)
    send = quarters[1:].astype(jnp.bfloat16)
    keep = (
        quarters[0]
        + exchanged(send[0], 0, 2).astype(jnp.float32)
        + exchanged(send[1], 1, 0).astype(jnp.float32)
        + exchanged(send[2], 1, 2).astype(jnp.float32)
    )
    send = keep.astype(jnp.bfloat16)
    total = keep[:each]
    for d in start_order(count):
        total = total + exchanged(send[d * each : (d + 1) * each], 0, 4 * d).astype(jnp.float32)
    return total.astype(jnp.bfloat16)


def body(gate_act, up_act, codes, scales):
    tensor_size = lax.axis_size("tensor")
    blocks = gate_act.shape[0] // HAD_LOCAL
    if (
        lax.axis_size("groups") == 2
        and tensor_size >= 4
        and blocks % 2 == 0
        and gate_act.shape[1] % tensor_size == 0
        and blocks * gate_act.shape[1] <= 128
        and codes.shape[1] % (16 * TILE) == 0
    ):
        return shared_body(gate_act, up_act, codes, scales)
    return general_body(gate_act, up_act, codes, scales)


def solution(mesh):
    placed = (P("tensor", "groups"), P("tensor", "groups"), P("tensor", None), P("tensor", None))
    return jax.shard_map(
        body, mesh=mesh, in_specs=placed, out_specs=P(("groups", "tensor"), None), check_vma=False
    )
```

```python
import functools
import math

import jax
import jax.numpy as jnp
import numpy as np
from jax import lax
from jax.experimental import pallas as pl
from jax.experimental.pallas import tpu as pltpu
from jax.sharding import PartitionSpec as P

HAD_CROSS = 128
GROUP = 32
HAD_LOCAL = 416
PAIRS = HAD_LOCAL // 2
WORDS_PER_GROUP = GROUP // 2
AXES = ("groups", "tensor")
MIB = 2**20
TILE = 512
CHUNK = 128
FETCHES = (1, 5, 4, 3)
LANES = 128


def paley_table():
    squares = set()
    for real_part in range(5):
        for root_part in range(5):
            squares.add(
                (
                    (real_part * real_part + 2 * root_part * root_part) % 5,
                    2 * real_part * root_part % 5,
                )
            )
    jacobsthal = np.zeros((25, 25))
    for first in range(25):
        for second in range(25):
            differ = ((first // 5 - second // 5) % 5, (first % 5 - second % 5) % 5)
            if differ == (0, 0):
                jacobsthal[first, second] = 0.0
            elif differ in squares:
                jacobsthal[first, second] = 1.0
            else:
                jacobsthal[first, second] = -1.0
    conference = np.zeros((26, 26))
    conference[0, 1:] = 1.0
    conference[1:, 0] = 1.0
    conference[1:, 1:] = jacobsthal
    return np.kron(conference, np.array([[1.0, 1.0], [1.0, -1.0]])) + np.kron(
        np.eye(26), np.array([[1.0, -1.0], [-1.0, -1.0]])
    )


def walsh_table(order):
    matrix = np.ones((1, 1))
    while matrix.shape[0] < order:
        matrix = np.kron(np.array([[1.0, 1.0], [1.0, -1.0]]), matrix)
    return matrix


def local_matrix(order):
    return np.kron(walsh_table(order // 52), paley_table()) / math.sqrt(order)


def hadamard_local(order):
    return jnp.asarray(local_matrix(order), dtype=jnp.float32).astype(jnp.bfloat16)


def sign_table(order):
    return jnp.asarray(walsh_table(order), dtype=jnp.float32)


def swapped(value, axis, distance):
    mask = 2**distance
    pairs = [(source, source ^ mask) for source in range(lax.axis_size(axis))]
    return lax.ppermute(value, axis, pairs)


def dequantize(words, group_scales):
    low_codes = words % 16
    high_codes = words // 16
    unpacked = jnp.stack([low_codes, high_codes], axis=1).reshape(
        2 * words.shape[0], words.shape[1]
    )
    spread = jnp.repeat(group_scales.astype(jnp.float32), GROUP, axis=0)
    return ((unpacked - 8).astype(jnp.float32) * spread).astype(jnp.bfloat16)


def general_body(gate_act, up_act, codes, scales):
    units_here = gate_act.shape[0]
    total_rows = gate_act.shape[1]
    blocks_here = units_here // HAD_LOCAL
    factor = 1.0 / math.sqrt(HAD_CROSS)
    hidden = (jax.nn.silu(gate_act.astype(jnp.float32)) * up_act.astype(jnp.float32)).astype(
        jnp.bfloat16
    )
    hidden = hidden.reshape(blocks_here, HAD_LOCAL, total_rows)
    local = jnp.einsum(
        "kn,anr->akr", hadamard_local(HAD_LOCAL), hidden, preferred_element_type=jnp.float32
    ).astype(jnp.bfloat16)
    partial_sums = jnp.einsum(
        "abr,ae->ebr",
        local.astype(jnp.float32),
        sign_table(blocks_here),
        precision=lax.Precision.HIGHEST,
    )
    my_index = lax.axis_index("tensor")
    for bit_pos in range(lax.axis_size("tensor").bit_length() - 1):
        partner = swapped(partial_sums, "tensor", bit_pos)
        upper = my_index // 2**bit_pos % 2
        partial_sums = jnp.where(upper == 0, partial_sums + partner, partner - partial_sums)
    rotated = (partial_sums * factor).astype(jnp.bfloat16)
    rotated = rotated.reshape(units_here, total_rows)
    weight = dequantize(codes, scales)
    summed = lax.psum_scatter(
        lax.dot_general(
            rotated, weight, (((0,), (0,)), ((), ())), preferred_element_type=jnp.float32
        ),
        "tensor",
        scatter_dimension=0,
        tiled=True,
    )
    return summed.astype(jnp.bfloat16)


def exchanged(value, group_mask, tensor_mask):
    tensor_size = lax.axis_size("tensor")
    pairs = [
        (g * tensor_size + t, (g ^ group_mask) * tensor_size + (t ^ tensor_mask))
        for g in range(lax.axis_size("groups"))
        for t in range(tensor_size)
    ]
    return lax.ppermute(value, AXES, pairs)


def start_order(count):
    return [count // 2] + [d for d in range(count - 1, 0, -1) if d != count // 2]


def middle_order(count):
    return list(range(count - 1, 0, -1))


def in_hbm(array):
    return pltpu.with_memory_space_constraint(array, pltpu.HBM)


def parity_sign(bits, masks):
    total = jnp.int32(0)
    position = 1
    while position <= masks:
        if masks & position:
            total = total + bits // position % 2
        position *= 2
    return (1 - 2 * (total % 2)).astype(jnp.float32)


def fetches(codes_hbm, group, first, count, words, sems, sem):
    height, tile = words.shape[1:]
    line = pl.multiple_of(group * height, height)
    return [
        pltpu.make_async_copy(
            codes_hbm.at[pl.ds(line, height), pl.ds((first + i) * tile, tile)],
            words.at[i],
            sems.at[sem + i],
        )
        for i in range(count)
    ]


def local_kernel(
    group_ref,
    gate_hbm,
    up_hbm,
    table_hbm,
    scales_hbm,
    out_ref,
    scales_ref,
    gate_in,
    up_in,
    table,
    hidden_sc,
    stack_sc,
    mix_sc,
    sems,
):
    group = group_ref[0]
    copies = [
        pltpu.make_async_copy(source, target, sems.at[index])
        for index, (source, target) in enumerate(
            ((gate_hbm, gate_in), (up_hbm, up_in), (table_hbm, table), (scales_hbm, scales_ref))
        )
    ]
    for copy in copies:
        copy.start()
    rows = gate_in.shape[0]
    blocks = gate_in.shape[1] // HAD_LOCAL
    half = blocks // 2
    line = lax.broadcasted_iota(jnp.int32, (blocks * rows, blocks * rows), 0)
    column = lax.broadcasted_iota(jnp.int32, (blocks * rows, blocks * rows), 1)
    common = (line // rows) & (column // rows)
    odd = jnp.zeros_like(common)
    for bit_pos in range(blocks.bit_length() - 1):
        odd = odd ^ ((common >> bit_pos) & 1)
    walsh = jnp.where(line % rows == column % rows, 1 - 2 * odd, 0)
    walsh = walsh.astype(jnp.float32).astype(jnp.bfloat16)
    copies[0].wait()
    copies[1].wait()
    gate = gate_in[...].astype(jnp.float32)
    hidden_sc[...] = gate / (1.0 + jnp.exp(-gate)) * up_in[...].astype(jnp.float32)
    for a in range(blocks):
        stack_sc[a * rows : (a + 1) * rows, :] = hidden_sc[
            :, a * HAD_LOCAL : (a + 1) * HAD_LOCAL
        ].astype(jnp.bfloat16)
    copies[2].wait()
    hidden = stack_sc[...]
    wide = table.shape[0] // HAD_LOCAL
    for piece in range(wide):
        local = jnp.dot(
            hidden,
            table[piece * HAD_LOCAL : (piece + 1) * HAD_LOCAL, :],
            preferred_element_type=jnp.float32,
        ).astype(jnp.bfloat16)
        mix_sc[:, piece * LANES : (piece + 1) * LANES] = jnp.dot(
            walsh, local, preferred_element_type=jnp.float32
        ).astype(jnp.bfloat16)
    padded = wide * LANES // 2
    for part in range(2):
        first = (group if part == 0 else 1 - group) * half
        for parity in range(2):
            for e in range(half):
                start = pl.multiple_of((first + e) * rows, rows)
                offset = (parity * half + e) * PAIRS
                out_ref[part, :, offset : offset + PAIRS] = mix_sc[
                    pl.ds(start, rows), parity * padded : parity * padded + PAIRS
                ]
    copies[3].wait()


def local_rotation(group, gate_act, up_act, scales):
    units, rows = gate_act.shape
    blocks = units // HAD_LOCAL
    padded = -(-PAIRS // LANES) * LANES
    by_parity = local_matrix(HAD_LOCAL).reshape(PAIRS, 2, HAD_LOCAL)
    table = np.zeros((HAD_LOCAL, 2 * padded), np.float32)
    table[:, :PAIRS] = by_parity[:, 0].T
    table[:, padded : padded + PAIRS] = by_parity[:, 1].T
    table = np.concatenate(np.split(table, 2 * padded // LANES, axis=1))
    hbm = pl.BlockSpec(memory_space=pltpu.HBM)
    vmem = pl.BlockSpec(memory_space=pltpu.VMEM)
    return pl.pallas_call(
        local_kernel,
        in_specs=[pl.BlockSpec(memory_space=pltpu.SMEM)] + [hbm] * 4,
        out_specs=[vmem, vmem],
        out_shape=[
            jax.ShapeDtypeStruct((2, rows, units // 2), jnp.bfloat16),
            pltpu.VMEM(scales.shape, scales.dtype),
        ],
        scratch_shapes=[
            pltpu.VMEM((rows, units), jnp.bfloat16),
            pltpu.VMEM((rows, units), jnp.bfloat16),
            pltpu.VMEM(table.shape, jnp.bfloat16),
            pltpu.VMEM((rows, units), jnp.float32),
            pltpu.VMEM((blocks * rows, HAD_LOCAL), jnp.bfloat16),
            pltpu.VMEM((blocks * rows, 2 * padded), jnp.bfloat16),
            pltpu.SemaphoreType.DMA((4,)),
        ],
        compiler_params=pltpu.CompilerParams(vmem_limit_bytes=6 * MIB),
        cost_estimate=pl.CostEstimate(flops=10**8, bytes_accessed=8 * MIB, transcendentals=10**5),
        name="local_rotation",
    )(
        group,
        in_hbm(gate_act.T),
        in_hbm(up_act.T),
        in_hbm(jnp.asarray(table, jnp.bfloat16)),
        in_hbm(scales),
    )


def unpack_span(words, scale):
    scale = jnp.broadcast_to(scale, words.shape).astype(jnp.bfloat16)
    eight = jnp.bfloat16(8)
    low = (words & 15).astype(jnp.float32).astype(jnp.bfloat16)
    high = (words >> 4).astype(jnp.float32).astype(jnp.bfloat16)
    return (low - eight) * scale, (high - eight) * scale


def widen(group, scales_ref, wide_ref):
    per = wide_ref.shape[0]
    for part in range(2):
        low = part * per // 16 * 16
        high = min(-(-(part + 1) * per // 16) * 16, scales_ref.shape[0])

        @pl.when(group == part)
        def _(part=part, low=low, high=high):
            wide = scales_ref[low:high, :].astype(jnp.float32)
            wide_ref[...] = wide[part * per - low : (part + 1) * per - low]


def unpack_tile(words, scales_ref, column, target, at, spans):
    height, tile = words.shape
    for p in spans:
        top = p * WORDS_PER_GROUP
        low, high = unpack_span(
            words[top : top + WORDS_PER_GROUP, :], scales_ref[p : p + 1, pl.ds(column, tile)]
        )
        target[top : top + WORDS_PER_GROUP, pl.ds(at, tile)] = low
        target[height + top : height + top + WORDS_PER_GROUP, pl.ds(at, tile)] = high


def first_kernel(group_ref, codes_hbm, scales_in, out_ref, next_ref, wide_ref, words, sems):
    group = group_ref[0]
    own, height, tile = words.shape
    ahead = next_ref.shape[0]
    copies = fetches(codes_hbm, group, 0, own, words, sems, 0)
    copies += fetches(codes_hbm, group, own, ahead, next_ref, sems, own)
    for copy in copies:
        copy.start()
    widen(group, scales_in, wide_ref)
    for i in range(own):
        copies[i].wait()
        unpack_tile(
            words.at[i], wide_ref, i * tile, out_ref, i * tile, range(height // WORDS_PER_GROUP)
        )
    for copy in copies[own:]:
        copy.wait()


def first_unpack(group, codes, scales, own, ahead):
    words, width = codes.shape
    hbm = pl.BlockSpec(memory_space=pltpu.HBM)
    vmem = pl.BlockSpec(memory_space=pltpu.VMEM)
    return pl.pallas_call(
        first_kernel,
        in_specs=[pl.BlockSpec(memory_space=pltpu.SMEM), hbm, vmem],
        out_specs=[vmem] * 3,
        out_shape=[
            pltpu.VMEM((words, own * TILE), jnp.bfloat16),
            pltpu.VMEM((ahead, words // 2, TILE), codes.dtype),
            pltpu.VMEM((words // 2 // WORDS_PER_GROUP, width), jnp.float32),
        ],
        scratch_shapes=[
            pltpu.VMEM((own, words // 2, TILE), codes.dtype),
            pltpu.SemaphoreType.DMA((own + ahead,)),
        ],
        compiler_params=pltpu.CompilerParams(vmem_limit_bytes=(2 + 2 * own) * MIB),
        cost_estimate=pl.CostEstimate(
            flops=0, bytes_accessed=(own + ahead) * words * TILE * 2, transcendentals=0
        ),
        name="first_unpack",
    )(group, in_hbm(codes), pltpu.with_memory_space_constraint(scales, pltpu.VMEM))


def unpack_kernel(first, group_ref, codes_hbm, scales_ref, given, out_ref, next_ref, words, sems):
    group = group_ref[0]
    count, height, tile = given.shape
    own, ahead = words.shape[0], next_ref.shape[0]
    copies = fetches(codes_hbm, group, first + count, own, words, sems, 0)
    copies += fetches(codes_hbm, group, first + count + own, ahead, next_ref, sems, own)
    for copy in copies:
        copy.start()
    spans = range(height // WORDS_PER_GROUP)

    @pl.loop(0, count)
    def _(i):
        at = pl.multiple_of(i * tile, tile)
        unpack_tile(given.at[i], scales_ref, first * tile + at, out_ref, at, spans)

    @pl.loop(0, own)
    def _(i):
        pltpu.make_async_copy(
            codes_hbm.at[pl.ds(0, height), pl.ds(0, tile)], words.at[i], sems.at[i]
        ).wait()
        at = pl.multiple_of((count + i) * tile, tile)
        unpack_tile(words.at[i], scales_ref, first * tile + at, out_ref, at, spans)

    for copy in copies[own:]:
        copy.wait()


def unpack(group, codes, scales, given, first, own, ahead):
    words = codes.shape[0]
    hbm = pl.BlockSpec(memory_space=pltpu.HBM)
    vmem = pl.BlockSpec(memory_space=pltpu.VMEM)
    columns = (given.shape[0] + own) * TILE
    return pl.pallas_call(
        functools.partial(unpack_kernel, first),
        in_specs=[pl.BlockSpec(memory_space=pltpu.SMEM), hbm, vmem, vmem],
        out_specs=[vmem, vmem],
        out_shape=[
            pltpu.VMEM((words, columns), jnp.bfloat16),
            pltpu.VMEM((ahead, words // 2, TILE), codes.dtype),
        ],
        scratch_shapes=[
            pltpu.VMEM((own, words // 2, TILE), codes.dtype),
            pltpu.SemaphoreType.DMA((own + ahead,)),
        ],
        compiler_params=pltpu.CompilerParams(vmem_limit_bytes=(2 + 2 * own) * MIB),
        cost_estimate=pl.CostEstimate(
            flops=words * columns * 8, bytes_accessed=words * columns * 4, transcendentals=0
        ),
        name="unpack",
    )(
        group,
        in_hbm(codes),
        pltpu.with_memory_space_constraint(scales, pltpu.VMEM),
        pltpu.with_memory_space_constraint(given, pltpu.VMEM),
    )


def product_kernel(readies, place_ref, codes_hbm, given, scales_ref, own_ref, *refs):
    *others, keep_ref, send_ref, first_sc, second_sc, words, sems = refs
    ready_refs, others = others[:readies], others[readies:]
    rows = own_ref.shape[0]
    group, place = place_ref[0], place_ref[1]
    held, height, tile = given.shape
    ready_tiles = [
        (ref, i * tile) for ref in ready_refs for i in range(ref.shape[1] // tile)
    ]
    tiles = scales_ref.shape[1] // tile
    base = len(ready_tiles)
    own = tiles - base - held
    copies = fetches(codes_hbm, group, base + held, own, words, sems, 0)
    for copy in copies:
        copy.start()

    count = len(others) + 1
    middle = 2 * (count - 1)
    total = own_ref[...].astype(jnp.float32) * parity_sign(place, middle)
    for distance, other in zip(middle_order(count), others):
        total = total + other[...].astype(jnp.float32) * parity_sign(
            place & (place ^ (2 * distance)), middle
        )
    rotated = (total * (1.0 / math.sqrt(HAD_CROSS))).astype(jnp.bfloat16)
    each = rows // (8 * count)
    slot = lax.broadcasted_iota(jnp.int32, (rows, rows), 0)
    column = lax.broadcasted_iota(jnp.int32, (rows, rows), 1)
    unit = slot // each
    away = unit // (4 * count) + 2 * (unit // count % 2) + 4 * (unit % count)
    source = (unit // (2 * count) % 2) * (rows // 2) + (away ^ place) * each + slot % each
    pick = (column == source).astype(jnp.float32).astype(jnp.bfloat16)
    rotated = jnp.dot(pick, rotated, preferred_element_type=jnp.float32).astype(jnp.bfloat16)

    depth = rotated.shape[1]
    spans = height // WORDS_PER_GROUP
    cuts = list(range(0, depth, CHUNK)) + [depth]

    def stage(products, fresh):
        sums = [None] * len(products)
        done = 0
        for k, (low, high) in enumerate(zip(cuts[:-1], cuts[1:])):
            for index, (weight, at, _) in enumerate(products):
                part = jnp.dot(
                    rotated[:, low:high],
                    weight[low:high, at : at + tile],
                    preferred_element_type=jnp.float32,
                )
                sums[index] = sums[index] + part if k else part
            if fresh is not None:
                source, column, target = fresh
                upto = spans * (k + 1) // (len(cuts) - 1)
                unpack_tile(source, scales_ref, column, target, 0, range(done, upto))
                done = upto
        for total, (_, _, to) in zip(sums, products):
            keep_ref[:, to : to + tile] = total[: rows // 2]
            send_ref[:, to : to + tile] = total[rows // 2 :].astype(jnp.bfloat16)

    waiting = [(ref, at, index * tile) for index, (ref, at) in enumerate(ready_tiles)]
    each_stage = -(-base // (tiles - base))
    previous = None
    for index in range(base, tiles):
        number = index - base
        if number >= held:
            copies[number - held].wait()
        source = given.at[number] if number < held else words.at[number - held]
        target = second_sc if number % 2 else first_sc
        products = waiting[:each_stage]
        waiting = waiting[each_stage:]
        if previous is not None:
            products.append(previous)
        stage(products, (source, index * tile, target))
        previous = (target, 0, index * tile)
    stage(waiting + [previous], None)


def product(place, codes, given, scales, own, others, ready):
    rows = own.shape[0]
    words, width = codes.shape
    hbm = pl.BlockSpec(memory_space=pltpu.HBM)
    vmem = pl.BlockSpec(memory_space=pltpu.VMEM)
    left = width // TILE - given.shape[0] - sum(r.shape[1] for r in ready) // TILE
    held = [pltpu.with_memory_space_constraint(r, pltpu.VMEM) for r in (given, scales)]
    return pl.pallas_call(
        functools.partial(product_kernel, len(ready)),
        in_specs=[pl.BlockSpec(memory_space=pltpu.SMEM), hbm]
        + [vmem] * (3 + len(ready) + len(others)),
        out_specs=[vmem, vmem],
        out_shape=[
            jax.ShapeDtypeStruct((rows // 2, width), jnp.float32),
            jax.ShapeDtypeStruct((rows // 2, width), jnp.bfloat16),
        ],
        scratch_shapes=[
            pltpu.VMEM((words, TILE), jnp.bfloat16),
            pltpu.VMEM((words, TILE), jnp.bfloat16),
            pltpu.VMEM((max(left, 1), words // 2, TILE), codes.dtype),
            pltpu.SemaphoreType.DMA((max(left, 1),)),
        ],
        compiler_params=pltpu.CompilerParams(vmem_limit_bytes=(8 + 2 * left) * MIB),
        name="product",
    )(
        place,
        in_hbm(codes),
        *held,
        own,
        *[pltpu.with_memory_space_constraint(r, pltpu.VMEM) for r in ready],
        *others,
    )


def shared_body(gate_act, up_act, codes, scales):
    rows = gate_act.shape[1]
    width = codes.shape[1]
    tensor_size = lax.axis_size("tensor")
    count = tensor_size // 4
    each = rows // tensor_size
    group = lax.axis_index("groups").astype(jnp.int32)[None]
    place = lax.axis_index("tensor").astype(jnp.int32)[None]

    tiles = width // TILE
    at_near, for_far, at_far, for_product = (tiles * n // 16 for n in FETCHES)
    parts, scales = local_rotation(group, gate_act, up_act, scales)
    near = exchanged(parts, 0, 1)
    core = place[0] % 2
    parts = jnp.where(
        core == 0,
        parts.astype(jnp.float32) + near.astype(jnp.float32),
        near.astype(jnp.float32) - parts.astype(jnp.float32),
    ).astype(jnp.bfloat16)
    parts, group_then = lax.optimization_barrier((parts, group))
    mine, theirs = parts[0], parts[1]
    top = tensor_size // 2
    across = exchanged(mine, 0, top).astype(jnp.float32)
    across_both = exchanged(theirs, 1, top).astype(jnp.float32)
    across_groups = exchanged(theirs, 1, 0).astype(jnp.float32)
    early, words, scales = first_unpack(group_then, codes, scales, at_near, for_far)
    sign = jnp.where(place[0] // top % 2 == 0, 1.0, -1.0)
    both = jnp.concatenate(
        [mine.astype(jnp.float32) * sign + across, across_both + across_groups * sign]
    ).astype(jnp.bfloat16)
    both, group_then, words = lax.optimization_barrier((both, group, words))
    others = [exchanged(both, 0, 2 * d) for d in middle_order(count)]
    late, words = unpack(group_then, codes, scales, words, at_near, at_far, for_product)
    keep, send = product(
        jnp.concatenate([group, place]), codes, words, scales, both, others, [early, late]
    )

    keep = keep + exchanged(send, 0, 1).astype(jnp.float32)
    quarters = keep.reshape(4, count * each, width)
    send = quarters[1:].astype(jnp.bfloat16)
    keep = (
        quarters[0]
        + exchanged(send[0], 0, 2).astype(jnp.float32)
        + exchanged(send[1], 1, 0).astype(jnp.float32)
        + exchanged(send[2], 1, 2).astype(jnp.float32)
    )
    send = keep.astype(jnp.bfloat16)
    total = keep[:each]
    for d in start_order(count):
        total = total + exchanged(send[d * each : (d + 1) * each], 0, 4 * d).astype(jnp.float32)
    return total.astype(jnp.bfloat16)


def body(gate_act, up_act, codes, scales):
    tensor_size = lax.axis_size("tensor")
    blocks = gate_act.shape[0] // HAD_LOCAL
    if (
        lax.axis_size("groups") == 2
        and tensor_size >= 4
        and blocks % 2 == 0
        and gate_act.shape[1] % tensor_size == 0
        and blocks * gate_act.shape[1] <= 128
        and codes.shape[1] % (16 * TILE) == 0
    ):
        return shared_body(gate_act, up_act, codes, scales)
    return general_body(gate_act, up_act, codes, scales)


def solution(mesh):
    placed = (P("tensor", "groups"), P("tensor", "groups"), P("tensor", None), P("tensor", None))
    return jax.shard_map(
        body, mesh=mesh, in_specs=placed, out_specs=P(("groups", "tensor"), None), check_vma=False
    )
```

```python
import functools
import math

import jax
import jax.numpy as jnp
import numpy as np
from jax import lax
from jax.experimental import pallas as pl
from jax.experimental.pallas import tpu as pltpu
from jax.sharding import PartitionSpec as P

HAD_CROSS = 128
GROUP = 32
HAD_LOCAL = 416
PAIRS = HAD_LOCAL // 2
WORDS_PER_GROUP = GROUP // 2
AXES = ("groups", "tensor")
MIB = 2**20
TILE = 512
CHUNK = 128
FETCHES = (1, 5, 4, 3)
LANES = 128


def paley_table():
    squares = set()
    for real_part in range(5):
        for root_part in range(5):
            squares.add(
                (
                    (real_part * real_part + 2 * root_part * root_part) % 5,
                    2 * real_part * root_part % 5,
                )
            )
    jacobsthal = np.zeros((25, 25))
    for first in range(25):
        for second in range(25):
            differ = ((first // 5 - second // 5) % 5, (first % 5 - second % 5) % 5)
            if differ == (0, 0):
                jacobsthal[first, second] = 0.0
            elif differ in squares:
                jacobsthal[first, second] = 1.0
            else:
                jacobsthal[first, second] = -1.0
    conference = np.zeros((26, 26))
    conference[0, 1:] = 1.0
    conference[1:, 0] = 1.0
    conference[1:, 1:] = jacobsthal
    return np.kron(conference, np.array([[1.0, 1.0], [1.0, -1.0]])) + np.kron(
        np.eye(26), np.array([[1.0, -1.0], [-1.0, -1.0]])
    )


def walsh_table(order):
    matrix = np.ones((1, 1))
    while matrix.shape[0] < order:
        matrix = np.kron(np.array([[1.0, 1.0], [1.0, -1.0]]), matrix)
    return matrix


def local_matrix(order):
    return np.kron(walsh_table(order // 52), paley_table()) / math.sqrt(order)


def hadamard_local(order):
    return jnp.asarray(local_matrix(order), dtype=jnp.float32).astype(jnp.bfloat16)


def sign_table(order):
    return jnp.asarray(walsh_table(order), dtype=jnp.float32)


def swapped(value, axis, distance):
    mask = 2**distance
    pairs = [(source, source ^ mask) for source in range(lax.axis_size(axis))]
    return lax.ppermute(value, axis, pairs)


def dequantize(words, group_scales):
    low_codes = words % 16
    high_codes = words // 16
    unpacked = jnp.stack([low_codes, high_codes], axis=1).reshape(
        2 * words.shape[0], words.shape[1]
    )
    spread = jnp.repeat(group_scales.astype(jnp.float32), GROUP, axis=0)
    return ((unpacked - 8).astype(jnp.float32) * spread).astype(jnp.bfloat16)


def general_body(gate_act, up_act, codes, scales):
    units_here = gate_act.shape[0]
    total_rows = gate_act.shape[1]
    blocks_here = units_here // HAD_LOCAL
    factor = 1.0 / math.sqrt(HAD_CROSS)
    hidden = (jax.nn.silu(gate_act.astype(jnp.float32)) * up_act.astype(jnp.float32)).astype(
        jnp.bfloat16
    )
    hidden = hidden.reshape(blocks_here, HAD_LOCAL, total_rows)
    local = jnp.einsum(
        "kn,anr->akr", hadamard_local(HAD_LOCAL), hidden, preferred_element_type=jnp.float32
    ).astype(jnp.bfloat16)
    partial_sums = jnp.einsum(
        "abr,ae->ebr",
        local.astype(jnp.float32),
        sign_table(blocks_here),
        precision=lax.Precision.HIGHEST,
    )
    my_index = lax.axis_index("tensor")
    for bit_pos in range(lax.axis_size("tensor").bit_length() - 1):
        partner = swapped(partial_sums, "tensor", bit_pos)
        upper = my_index // 2**bit_pos % 2
        partial_sums = jnp.where(upper == 0, partial_sums + partner, partner - partial_sums)
    rotated = (partial_sums * factor).astype(jnp.bfloat16)
    rotated = rotated.reshape(units_here, total_rows)
    weight = dequantize(codes, scales)
    summed = lax.psum_scatter(
        lax.dot_general(
            rotated, weight, (((0,), (0,)), ((), ())), preferred_element_type=jnp.float32
        ),
        "tensor",
        scatter_dimension=0,
        tiled=True,
    )
    return summed.astype(jnp.bfloat16)


def exchanged(value, group_mask, tensor_mask):
    tensor_size = lax.axis_size("tensor")
    pairs = [
        (g * tensor_size + t, (g ^ group_mask) * tensor_size + (t ^ tensor_mask))
        for g in range(lax.axis_size("groups"))
        for t in range(tensor_size)
    ]
    return lax.ppermute(value, AXES, pairs)


def start_order(count):
    return [count // 2] + [d for d in range(count - 1, 0, -1) if d != count // 2]


def middle_order(count):
    return list(range(count - 1, 0, -1))


def in_hbm(array):
    return pltpu.with_memory_space_constraint(array, pltpu.HBM)


def parity_sign(bits, masks):
    total = jnp.int32(0)
    position = 1
    while position <= masks:
        if masks & position:
            total = total + bits // position % 2
        position *= 2
    return (1 - 2 * (total % 2)).astype(jnp.float32)


def fetches(codes_hbm, group, first, count, words, sems, sem):
    height, tile = words.shape[1:]
    line = pl.multiple_of(group * height, height)
    return [
        pltpu.make_async_copy(
            codes_hbm.at[pl.ds(line, height), pl.ds((first + i) * tile, tile)],
            words.at[i],
            sems.at[sem + i],
        )
        for i in range(count)
    ]


def local_kernel(
    group_ref,
    gate_hbm,
    up_hbm,
    table_hbm,
    scales_hbm,
    out_ref,
    scales_ref,
    gate_in,
    up_in,
    table,
    hidden_sc,
    stack_sc,
    mix_sc,
    sems,
):
    group = group_ref[0]
    copies = [
        pltpu.make_async_copy(source, target, sems.at[index])
        for index, (source, target) in enumerate(
            ((gate_hbm, gate_in), (up_hbm, up_in), (table_hbm, table), (scales_hbm, scales_ref))
        )
    ]
    for copy in copies:
        copy.start()
    rows = gate_in.shape[0]
    blocks = gate_in.shape[1] // HAD_LOCAL
    half = blocks // 2
    line = lax.broadcasted_iota(jnp.int32, (blocks * rows, blocks * rows), 0)
    column = lax.broadcasted_iota(jnp.int32, (blocks * rows, blocks * rows), 1)
    common = (line // rows) & (column // rows)
    odd = jnp.zeros_like(common)
    for bit_pos in range(blocks.bit_length() - 1):
        odd = odd ^ ((common >> bit_pos) & 1)
    walsh = jnp.where(line % rows == column % rows, 1 - 2 * odd, 0)
    walsh = walsh.astype(jnp.float32).astype(jnp.bfloat16)
    copies[0].wait()
    copies[1].wait()
    gate = gate_in[...].astype(jnp.float32)
    hidden_sc[...] = gate / (1.0 + jnp.exp(-gate)) * up_in[...].astype(jnp.float32)
    for a in range(blocks):
        stack_sc[a * rows : (a + 1) * rows, :] = hidden_sc[
            :, a * HAD_LOCAL : (a + 1) * HAD_LOCAL
        ].astype(jnp.bfloat16)
    copies[2].wait()
    hidden = stack_sc[...]
    wide = table.shape[0] // HAD_LOCAL
    for piece in range(wide):
        local = jnp.dot(
            hidden,
            table[piece * HAD_LOCAL : (piece + 1) * HAD_LOCAL, :],
            preferred_element_type=jnp.float32,
        ).astype(jnp.bfloat16)
        mix_sc[:, piece * LANES : (piece + 1) * LANES] = jnp.dot(
            walsh, local, preferred_element_type=jnp.float32
        ).astype(jnp.bfloat16)
    padded = wide * LANES // 2
    for part in range(2):
        first = (group if part == 0 else 1 - group) * half
        for parity in range(2):
            for e in range(half):
                start = pl.multiple_of((first + e) * rows, rows)
                offset = (parity * half + e) * PAIRS
                out_ref[part, :, offset : offset + PAIRS] = mix_sc[
                    pl.ds(start, rows), parity * padded : parity * padded + PAIRS
                ]
    copies[3].wait()


def local_rotation(group, gate_act, up_act, scales):
    units, rows = gate_act.shape
    blocks = units // HAD_LOCAL
    padded = -(-PAIRS // LANES) * LANES
    by_parity = local_matrix(HAD_LOCAL).reshape(PAIRS, 2, HAD_LOCAL)
    table = np.zeros((HAD_LOCAL, 2 * padded), np.float32)
    table[:, :PAIRS] = by_parity[:, 0].T
    table[:, padded : padded + PAIRS] = by_parity[:, 1].T
    table = np.concatenate(np.split(table, 2 * padded // LANES, axis=1))
    hbm = pl.BlockSpec(memory_space=pltpu.HBM)
    vmem = pl.BlockSpec(memory_space=pltpu.VMEM)
    return pl.pallas_call(
        local_kernel,
        in_specs=[pl.BlockSpec(memory_space=pltpu.SMEM)] + [hbm] * 4,
        out_specs=[vmem, vmem],
        out_shape=[
            jax.ShapeDtypeStruct((2, rows, units // 2), jnp.bfloat16),
            pltpu.VMEM(scales.shape, scales.dtype),
        ],
        scratch_shapes=[
            pltpu.VMEM((rows, units), jnp.bfloat16),
            pltpu.VMEM((rows, units), jnp.bfloat16),
            pltpu.VMEM(table.shape, jnp.bfloat16),
            pltpu.VMEM((rows, units), jnp.float32),
            pltpu.VMEM((blocks * rows, HAD_LOCAL), jnp.bfloat16),
            pltpu.VMEM((blocks * rows, 2 * padded), jnp.bfloat16),
            pltpu.SemaphoreType.DMA((4,)),
        ],
        compiler_params=pltpu.CompilerParams(vmem_limit_bytes=6 * MIB),
        cost_estimate=pl.CostEstimate(flops=10**8, bytes_accessed=8 * MIB, transcendentals=10**5),
        name="local_rotation",
    )(
        group,
        in_hbm(gate_act.T),
        in_hbm(up_act.T),
        in_hbm(jnp.asarray(table, jnp.bfloat16)),
        in_hbm(scales),
    )


def unpack_span(words, scale):
    scale = jnp.broadcast_to(scale, words.shape).astype(jnp.bfloat16)
    eight = jnp.bfloat16(8)
    low = (words & 15).astype(jnp.float32).astype(jnp.bfloat16)
    high = (words >> 4).astype(jnp.float32).astype(jnp.bfloat16)
    return (low - eight) * scale, (high - eight) * scale


def widen(group, scales_ref, wide_ref):
    per = wide_ref.shape[0]
    for part in range(2):
        low = part * per // 16 * 16
        high = min(-(-(part + 1) * per // 16) * 16, scales_ref.shape[0])

        @pl.when(group == part)
        def _(part=part, low=low, high=high):
            wide = scales_ref[low:high, :].astype(jnp.float32)
            wide_ref[...] = wide[part * per - low : (part + 1) * per - low]


def unpack_tile(words, scales_ref, column, target, at, spans):
    height, tile = words.shape
    for p in spans:
        top = p * WORDS_PER_GROUP
        low, high = unpack_span(
            words[top : top + WORDS_PER_GROUP, :], scales_ref[p : p + 1, pl.ds(column, tile)]
        )
        target[top : top + WORDS_PER_GROUP, pl.ds(at, tile)] = low
        target[height + top : height + top + WORDS_PER_GROUP, pl.ds(at, tile)] = high


def first_kernel(group_ref, codes_hbm, scales_in, out_ref, next_ref, wide_ref, words, sems):
    group = group_ref[0]
    own, height, tile = words.shape
    ahead = next_ref.shape[0]
    copies = fetches(codes_hbm, group, 0, own, words, sems, 0)
    copies += fetches(codes_hbm, group, own, ahead, next_ref, sems, own)
    for copy in copies:
        copy.start()
    widen(group, scales_in, wide_ref)
    for i in range(own):
        copies[i].wait()
        unpack_tile(
            words.at[i], wide_ref, i * tile, out_ref, i * tile, range(height // WORDS_PER_GROUP)
        )
    for copy in copies[own:]:
        copy.wait()


def first_unpack(group, codes, scales, own, ahead):
    words, width = codes.shape
    hbm = pl.BlockSpec(memory_space=pltpu.HBM)
    vmem = pl.BlockSpec(memory_space=pltpu.VMEM)
    return pl.pallas_call(
        first_kernel,
        in_specs=[pl.BlockSpec(memory_space=pltpu.SMEM), hbm, vmem],
        out_specs=[vmem] * 3,
        out_shape=[
            pltpu.VMEM((words, own * TILE), jnp.bfloat16),
            pltpu.VMEM((ahead, words // 2, TILE), codes.dtype),
            pltpu.VMEM((words // 2 // WORDS_PER_GROUP, width), jnp.float32),
        ],
        scratch_shapes=[
            pltpu.VMEM((own, words // 2, TILE), codes.dtype),
            pltpu.SemaphoreType.DMA((own + ahead,)),
        ],
        compiler_params=pltpu.CompilerParams(vmem_limit_bytes=(2 + 2 * own) * MIB),
        cost_estimate=pl.CostEstimate(
            flops=0, bytes_accessed=(own + ahead) * words * TILE * 2, transcendentals=0
        ),
        name="first_unpack",
    )(group, in_hbm(codes), pltpu.with_memory_space_constraint(scales, pltpu.VMEM))


def unpack_kernel(first, group_ref, codes_hbm, scales_ref, given, out_ref, next_ref, words, sems):
    group = group_ref[0]
    count, height, tile = given.shape
    own, ahead = words.shape[0], next_ref.shape[0]
    copies = fetches(codes_hbm, group, first + count, own, words, sems, 0)
    copies += fetches(codes_hbm, group, first + count + own, ahead, next_ref, sems, own)
    for copy in copies:
        copy.start()
    spans = range(height // WORDS_PER_GROUP)

    @pl.loop(0, count)
    def _(i):
        at = pl.multiple_of(i * tile, tile)
        unpack_tile(given.at[i], scales_ref, first * tile + at, out_ref, at, spans)

    @pl.loop(0, own)
    def _(i):
        pltpu.make_async_copy(
            codes_hbm.at[pl.ds(0, height), pl.ds(0, tile)], words.at[i], sems.at[i]
        ).wait()
        at = pl.multiple_of((count + i) * tile, tile)
        unpack_tile(words.at[i], scales_ref, first * tile + at, out_ref, at, spans)

    for copy in copies[own:]:
        copy.wait()


def unpack(group, codes, scales, given, first, own, ahead):
    words = codes.shape[0]
    hbm = pl.BlockSpec(memory_space=pltpu.HBM)
    vmem = pl.BlockSpec(memory_space=pltpu.VMEM)
    columns = (given.shape[0] + own) * TILE
    return pl.pallas_call(
        functools.partial(unpack_kernel, first),
        in_specs=[pl.BlockSpec(memory_space=pltpu.SMEM), hbm, vmem, vmem],
        out_specs=[vmem, vmem],
        out_shape=[
            pltpu.VMEM((words, columns), jnp.bfloat16),
            pltpu.VMEM((ahead, words // 2, TILE), codes.dtype),
        ],
        scratch_shapes=[
            pltpu.VMEM((own, words // 2, TILE), codes.dtype),
            pltpu.SemaphoreType.DMA((own + ahead,)),
        ],
        compiler_params=pltpu.CompilerParams(vmem_limit_bytes=(2 + 2 * own) * MIB),
        cost_estimate=pl.CostEstimate(
            flops=words * columns * 8, bytes_accessed=words * columns * 4, transcendentals=0
        ),
        name="unpack",
    )(
        group,
        in_hbm(codes),
        pltpu.with_memory_space_constraint(scales, pltpu.VMEM),
        pltpu.with_memory_space_constraint(given, pltpu.VMEM),
    )


def product_kernel(readies, place_ref, codes_hbm, given, scales_ref, own_ref, *refs):
    *others, keep_ref, send_ref, first_sc, second_sc, words, sems = refs
    ready_refs, others = others[:readies], others[readies:]
    rows = own_ref.shape[0]
    group, place = place_ref[0], place_ref[1]
    held, height, tile = given.shape
    ready_tiles = [
        (ref, i * tile) for ref in ready_refs for i in range(ref.shape[1] // tile)
    ]
    tiles = scales_ref.shape[1] // tile
    base = len(ready_tiles)
    own = tiles - base - held
    copies = fetches(codes_hbm, group, base + held, own, words, sems, 0)
    for copy in copies:
        copy.start()

    unpack_tile(
        given.at[0], scales_ref, base * tile, first_sc, 0, range(height // WORDS_PER_GROUP)
    )
    count = len(others) + 1
    middle = 2 * (count - 1)
    total = own_ref[...].astype(jnp.float32) * parity_sign(place, middle)
    for distance, other in zip(middle_order(count), others):
        total = total + other[...].astype(jnp.float32) * parity_sign(
            place & (place ^ (2 * distance)), middle
        )
    rotated = (total * (1.0 / math.sqrt(HAD_CROSS))).astype(jnp.bfloat16)
    each = rows // (8 * count)
    slot = lax.broadcasted_iota(jnp.int32, (rows, rows), 0)
    column = lax.broadcasted_iota(jnp.int32, (rows, rows), 1)
    unit = slot // each
    away = unit // (4 * count) + 2 * (unit // count % 2) + 4 * (unit % count)
    source = (unit // (2 * count) % 2) * (rows // 2) + (away ^ place) * each + slot % each
    pick = (column == source).astype(jnp.float32).astype(jnp.bfloat16)
    rotated = jnp.dot(pick, rotated, preferred_element_type=jnp.float32).astype(jnp.bfloat16)

    depth = rotated.shape[1]
    spans = height // WORDS_PER_GROUP
    cuts = list(range(0, depth, CHUNK)) + [depth]

    def stage(products, fresh):
        sums = [None] * len(products)
        done = 0
        for k, (low, high) in enumerate(zip(cuts[:-1], cuts[1:])):
            for index, (weight, at, _) in enumerate(products):
                part = jnp.dot(
                    rotated[:, low:high],
                    weight[low:high, at : at + tile],
                    preferred_element_type=jnp.float32,
                )
                sums[index] = sums[index] + part if k else part
            if fresh is not None:
                source, column, target = fresh
                upto = spans * (k + 1) // (len(cuts) - 1)
                unpack_tile(source, scales_ref, column, target, 0, range(done, upto))
                done = upto
        for total, (_, _, to) in zip(sums, products):
            keep_ref[:, to : to + tile] = total[: rows // 2]
            send_ref[:, to : to + tile] = total[rows // 2 :].astype(jnp.bfloat16)

    waiting = [(ref, at, index * tile) for index, (ref, at) in enumerate(ready_tiles)]
    each_stage = -(-base // (tiles - base - 1))
    previous = (first_sc, 0, base * tile)
    for index in range(base + 1, tiles):
        number = index - base
        if number >= held:
            copies[number - held].wait()
        source = given.at[number] if number < held else words.at[number - held]
        target = second_sc if number % 2 else first_sc
        products = waiting[:each_stage]
        waiting = waiting[each_stage:]
        products.append(previous)
        stage(products, (source, index * tile, target))
        previous = (target, 0, index * tile)
    stage(waiting + [previous], None)


def product(place, codes, given, scales, own, others, ready):
    rows = own.shape[0]
    words, width = codes.shape
    hbm = pl.BlockSpec(memory_space=pltpu.HBM)
    vmem = pl.BlockSpec(memory_space=pltpu.VMEM)
    left = width // TILE - given.shape[0] - sum(r.shape[1] for r in ready) // TILE
    held = [pltpu.with_memory_space_constraint(r, pltpu.VMEM) for r in (given, scales)]
    return pl.pallas_call(
        functools.partial(product_kernel, len(ready)),
        in_specs=[pl.BlockSpec(memory_space=pltpu.SMEM), hbm]
        + [vmem] * (3 + len(ready) + len(others)),
        out_specs=[vmem, vmem],
        out_shape=[
            jax.ShapeDtypeStruct((rows // 2, width), jnp.float32),
            jax.ShapeDtypeStruct((rows // 2, width), jnp.bfloat16),
        ],
        scratch_shapes=[
            pltpu.VMEM((words, TILE), jnp.bfloat16),
            pltpu.VMEM((words, TILE), jnp.bfloat16),
            pltpu.VMEM((max(left, 1), words // 2, TILE), codes.dtype),
            pltpu.SemaphoreType.DMA((max(left, 1),)),
        ],
        compiler_params=pltpu.CompilerParams(vmem_limit_bytes=(8 + 2 * left) * MIB),
        name="product",
    )(
        place,
        in_hbm(codes),
        *held,
        own,
        *[pltpu.with_memory_space_constraint(r, pltpu.VMEM) for r in ready],
        *others,
    )


def shared_body(gate_act, up_act, codes, scales):
    rows = gate_act.shape[1]
    width = codes.shape[1]
    tensor_size = lax.axis_size("tensor")
    count = tensor_size // 4
    each = rows // tensor_size
    group = lax.axis_index("groups").astype(jnp.int32)[None]
    place = lax.axis_index("tensor").astype(jnp.int32)[None]

    tiles = width // TILE
    at_near, for_far, at_far, for_product = (tiles * n // 16 for n in FETCHES)
    parts, scales = local_rotation(group, gate_act, up_act, scales)
    near = exchanged(parts, 0, 1)
    core = place[0] % 2
    parts = jnp.where(
        core == 0,
        parts.astype(jnp.float32) + near.astype(jnp.float32),
        near.astype(jnp.float32) - parts.astype(jnp.float32),
    ).astype(jnp.bfloat16)
    parts, group_then = lax.optimization_barrier((parts, group))
    mine, theirs = parts[0], parts[1]
    top = tensor_size // 2
    across = exchanged(mine, 0, top).astype(jnp.float32)
    across_both = exchanged(theirs, 1, top).astype(jnp.float32)
    across_groups = exchanged(theirs, 1, 0).astype(jnp.float32)
    early, words, scales = first_unpack(group_then, codes, scales, at_near, for_far)
    sign = jnp.where(place[0] // top % 2 == 0, 1.0, -1.0)
    both = jnp.concatenate(
        [mine.astype(jnp.float32) * sign + across, across_both + across_groups * sign]
    ).astype(jnp.bfloat16)
    both, group_then, words = lax.optimization_barrier((both, group, words))
    others = [exchanged(both, 0, 2 * d) for d in middle_order(count)]
    late, words = unpack(group_then, codes, scales, words, at_near, at_far, for_product)
    keep, send = product(
        jnp.concatenate([group, place]), codes, words, scales, both, others, [early, late]
    )

    keep = keep + exchanged(send, 0, 1).astype(jnp.float32)
    quarters = keep.reshape(4, count * each, width)
    send = quarters[1:].astype(jnp.bfloat16)
    keep = (
        quarters[0]
        + exchanged(send[0], 0, 2).astype(jnp.float32)
        + exchanged(send[1], 1, 0).astype(jnp.float32)
        + exchanged(send[2], 1, 2).astype(jnp.float32)
    )
    send = keep.astype(jnp.bfloat16)
    total = keep[:each]
    for d in start_order(count):
        total = total + exchanged(send[d * each : (d + 1) * each], 0, 4 * d).astype(jnp.float32)
    return total.astype(jnp.bfloat16)


def body(gate_act, up_act, codes, scales):
    tensor_size = lax.axis_size("tensor")
    blocks = gate_act.shape[0] // HAD_LOCAL
    if (
        lax.axis_size("groups") == 2
        and tensor_size >= 4
        and blocks % 2 == 0
        and gate_act.shape[1] % tensor_size == 0
        and blocks * gate_act.shape[1] <= 128
        and codes.shape[1] % (16 * TILE) == 0
    ):
        return shared_body(gate_act, up_act, codes, scales)
    return general_body(gate_act, up_act, codes, scales)


def solution(mesh):
    placed = (P("tensor", "groups"), P("tensor", "groups"), P("tensor", None), P("tensor", None))
    return jax.shard_map(
        body, mesh=mesh, in_specs=placed, out_specs=P(("groups", "tensor"), None), check_vma=False
    )
```
